128 devices in a mesh: seq: 32 (over z, y, core), head: 4 (over x).
Axes of the slice: x: 4, y: 4, z: 4, core: 2. Of those that a mesh axis runs over, the one named last changes fastest.
Arguments:
- queries: bfloat16 [32768, 2560], P(('seq', 'head'))
- keys: bfloat16 [32768, 2560], P(('seq', 'head'))
- values: bfloat16 [32768, 2560], P(('seq', 'head')), may hold values from -6 to 6
- gain_q: float32 [2560], replicated, may hold values from 0.1 to 1.9
- gain_k: float32 [2560], replicated, may hold values from 0.1 to 1.9
- key_tiles: int32 [256, 18], replicated, may hold values from 0 to 255, as said below
- tile_counts: int32 [256], replicated, may hold values from 1 to 18
- tile_valid: int32 [256], replicated, may hold values from 1 to 128, as said below
Outputs:
- attended: bfloat16 [32768, 2560], P(('seq', 'head'))
The draws below stay inside these ranges and needn't reach their ends.
Inputs may be any that keep to these rules, and one draw needn't show every extreme that they name: `key_tiles`: entry 0 of row i is i and entry 1 is the other tile of the pair (2 m, 2 m + 1) holding i; the entries of a row are distinct tiles. Counting blocks of 8 tiles, the used entries of all rows of one block name at most one tile of each other block. `tile_valid`: every tile but the last one is full.
All inputs are finite; a program needn't handle non-finite values.
Results may differ from the reference program's by a relative error of at most 0.0072.
Values may be sent and summed in bfloat16 or wider, within the bound.
A program may use at most 192 MiB of HBM per device.

```python
import jax
import jax.numpy as jnp
from jax import lax

HEADS = 20
HD = 128
TILE = 128
HW = 2560
SPAN_TILES = 8
NTILES = 256
TOKENS = 32768
FAR = 16
KMAX = 18
N_SEQ = 32


def draw_queries(key, part):
    key = jax.random.fold_in(key, 21)
    base = jnp.clip(jax.random.normal(key, (TOKENS, HW), jnp.float32), -6.0, 6.0)
    return base.astype(jnp.bfloat16)


def draw_keys(key, part):
    key = jax.random.fold_in(key, 22)
    base = jnp.clip(jax.random.normal(key, (TOKENS, HW), jnp.float32), -6.0, 6.0)
    return base.astype(jnp.bfloat16)


def draw_key_tiles(key, part):
    key = jax.random.fold_in(key, 11)
    pick = jax.random.randint(key, (N_SEQ, N_SEQ), 0, SPAN_TILES)
    tile = jnp.arange(NTILES, dtype=jnp.int32)
    span = tile // SPAN_TILES
    row = tile % SPAN_TILES
    far = jnp.arange(FAR, dtype=jnp.int32)
    owner = (span[:, None] + 1 + (row[:, None] * FAR + far[None, :]) % (N_SEQ - 1)) % N_SEQ
    far_tiles = owner * SPAN_TILES + pick[span[:, None], owner]
    partner = span * SPAN_TILES + row + 1 - 2 * (row % 2)
    return jnp.concatenate([tile[:, None], partner[:, None], far_tiles], axis=1).astype(jnp.int32)


def draw_tile_counts(key, part):
    key = jax.random.fold_in(key, 12)
    first, second, third, fourth = jax.random.split(key, 4)
    span_ids = jnp.arange(N_SEQ, dtype=jnp.int32)
    forced = jax.random.randint(fourth, (), 0, N_SEQ)
    heavy = (jax.random.randint(first, (N_SEQ,), 0, 4) == 0) | (span_ids == forced)
    tile = jnp.arange(NTILES, dtype=jnp.int32)
    high = jax.random.randint(second, (NTILES,), KMAX - 2, KMAX + 1)
    low = jax.random.randint(third, (NTILES,), 1, KMAX // 2 + 1)
    counts = jnp.where(heavy[tile // SPAN_TILES], high, low)
    counts = jnp.where(tile == forced * SPAN_TILES, KMAX, counts)
    return counts.astype(jnp.int32)


def draw_tile_valid(key, part):
    key = jax.random.fold_in(key, 13)
    last = jax.random.randint(key, (), 1, TILE + 1)
    tile = jnp.arange(NTILES, dtype=jnp.int32)
    return jnp.where(tile == NTILES - 1, last, TILE).astype(jnp.int32)


def shard_levels(own_key, dims, cuts, low, largest):
    level, own = 1.0, jax.random.fold_in(own_key, 6)
    for dim, parts in cuts:
        steps = jnp.exp(jax.random.uniform(jax.random.fold_in(own, dim), (parts,), jnp.float32, low / len(cuts), largest / len(cuts)))
        level = level * jnp.repeat(steps, dims[dim] // parts).reshape([-1 if axis == dim else 1 for axis in range(len(dims))])
    return level


def gaussian(own_key, dims, scale, limit, pieces=(), kind=jnp.bfloat16):
    drawn = scale * jax.random.normal(own_key, dims, jnp.float32)
    if pieces:
        drawn = drawn * shard_levels(own_key, dims, pieces, -0.22, 0.18)
    return jnp.clip(drawn, -limit, limit).astype(kind)


def setup_inputs(seed: int = 0) -> dict:
    seeds = jax.random.split(jax.random.key(seed), 9)
    return {
        "queries": draw_queries(jax.random.fold_in(seeds[8], 71), 0),
        "keys": draw_keys(jax.random.fold_in(seeds[8], 71), 0),
        "values": gaussian(seeds[2], (TOKENS, HW), 1.0, 6.0, ((0, 128),)),
        "gain_q": jnp.clip(1.0 + 0.18 * jax.random.normal(seeds[3], (HW,), jnp.float32), 0.1, 1.9),
        "gain_k": jnp.clip(1.0 + 0.18 * jax.random.normal(seeds[4], (HW,), jnp.float32), 0.1, 1.9),
        "key_tiles": draw_key_tiles(jax.random.fold_in(seeds[8], 71), 0),
        "tile_counts": draw_tile_counts(jax.random.fold_in(seeds[8], 71), 0),
        "tile_valid": draw_tile_valid(jax.random.fold_in(seeds[8], 71), 0),
    }


def normalize_rows(rows, gain):
    values_f = rows.astype(jnp.float32)
    scale = lax.rsqrt(lax.optimization_barrier(jnp.sum(values_f * values_f, axis=-1, keepdims=True)) / HW + 1e-06)
    return (values_f * scale * gain).astype(jnp.bfloat16)

def reference(queries, keys, values, gain_q, gain_k, key_tiles, tile_counts, tile_valid):
    q_norm = normalize_rows(queries, gain_q).reshape(NTILES, TILE, HEADS, HD)
    k_norm = normalize_rows(keys, gain_k).reshape(NTILES, TILE, HEADS, HD)
    v_all = values.reshape(NTILES, TILE, HEADS, HD)
    slot_ids = jnp.arange(KMAX, dtype=jnp.int32)
    position = jnp.arange(TILE, dtype=jnp.int32)

    def one_tile(tile):
        chosen = key_tiles[tile].astype(jnp.int32)
        k_sel = jnp.take(k_norm, chosen, axis=0).astype(jnp.float32)
        v_sel = jnp.take(v_all, chosen, axis=0).astype(jnp.float32)
        keep = (slot_ids < tile_counts[tile])[:, None] & (position[None, :] < jnp.take(tile_valid, chosen)[:, None])
        query_f = q_norm[tile].astype(jnp.float32)
        scores = jnp.einsum('ahd,kbhd->hakb', query_f, k_sel) * HD ** (-0.5)
        scores = jnp.where(keep[None, None, :, :], scores, -1e+30)
        peak = lax.optimization_barrier(jnp.max(scores, axis=(2, 3), keepdims=True))
        weights = jnp.exp(scores - peak).astype(jnp.bfloat16)
        weights_f = weights.astype(jnp.float32)
        total = lax.optimization_barrier(jnp.sum(weights_f, axis=(2, 3)))
        mixed = jnp.einsum('hakb,kbhd->ahd', weights_f, v_sel)
        return (mixed / jnp.transpose(total)[:, :, None]).astype(jnp.bfloat16)
    result = lax.map(one_tile, jnp.arange(NTILES, dtype=jnp.int32))
    return result.reshape(TOKENS, HW)
```

```python
import functools
import math

import jax
import jax.numpy as jnp
from jax import lax
from jax.experimental import pallas as pl
from jax.experimental.pallas import tpu as pltpu
from jax.sharding import PartitionSpec as P

HD = 128
TILE = 128
EPS = 1e-06
MASKED = -1e30
MESH = pl.DeviceIdType.MESH
LOG2E = math.log2(math.e)


def row_scale(rows_ref, width):
    groups = width // HD
    total = jnp.zeros((rows_ref.shape[0], TILE, HD), jnp.float32)
    for g in range(groups):
        part = rows_ref[:, :, g * HD : (g + 1) * HD].astype(jnp.float32)
        total = total + part * part
    return lax.rsqrt(jnp.sum(total, axis=-1, keepdims=True) / width + EPS)


def kernel(
    n_seq, n_head, heads_here,
    wanted, listed, counts, valid, q_hbm, k_hbm, v_hbm, gain_q, gain_k,
    o_hbm,
    q_in, k_in, q_stage, k_stage, send, out_stage, *rest,
):
    q_blk = rest[:heads_here]
    k_blk = rest[heads_here : 2 * heads_here]
    v_blk = rest[2 * heads_here : 3 * heads_here]
    bank = rest[3 * heads_here : 4 * heads_here]
    (in_sem, own_sem, a_send, a_recv, b_send, b_recv, o_send, o_recv, o_own) = rest[4 * heads_here :]
    s = lax.axis_index("seq")
    x = lax.axis_index("head")
    own_tiles = q_hbm.shape[0]
    span_tiles = own_tiles * n_head
    width = q_hbm.shape[2]
    slots = listed.shape[1]
    mine = pl.ds(x * own_tiles, own_tiles)

    load_k = pltpu.make_async_copy(k_hbm, k_in, in_sem.at[0])
    load_q = pltpu.make_async_copy(q_hbm, q_in, in_sem.at[1])
    load_k.start()
    load_q.start()

    def columns(head):
        return pl.ds(pl.multiple_of(head * HD, HD), HD)

    own_v = []
    for h in range(heads_here):
        copy = pltpu.make_async_copy(
            v_hbm.at[:, :, columns(x * heads_here + h)], v_blk[h].at[mine], own_sem.at[h]
        )
        copy.start()
        own_v.append(copy)

    barrier = pltpu.get_barrier_semaphore()
    for o in range(1, n_head):
        pl.semaphore_signal(
            barrier, inc=1, device_id=(s, lax.rem(x + o, n_head)), device_id_type=MESH
        )

    @pl.loop(1, n_seq)
    def _(d):
        pl.semaphore_signal(
            barrier, inc=1, device_id=(lax.rem(s + d, n_seq), x), device_id_type=MESH
        )

    load_k.wait()
    k_scale = row_scale(k_in, width)
    pl.semaphore_wait(barrier, n_head + n_seq - 2)

    def to_head(kind, h, o, src, dst):
        return pltpu.make_async_remote_copy(
            src_ref=src,
            dst_ref=dst.at[mine],
            send_sem=a_send.at[kind],
            recv_sem=a_recv.at[kind, h, o - 1],
            device_id=(s, lax.rem(x + o, n_head)),
            device_id_type=MESH,
        )

    def spread(kind, h, rows_in, scale, gain, stage, blocks):
        for o in (2, 1, 3, 0):
            cols = columns(lax.rem(x + o, n_head) * heads_here + h)
            rows = rows_in[:, :, cols].astype(jnp.float32)
            rows = (rows * scale * gain[:, cols][None]).astype(jnp.bfloat16)
            if o == 0:
                blocks[h][mine] = rows
            else:
                stage[o - 1, h] = rows
                to_head(kind, h, o, stage.at[o - 1, h], blocks[h]).start()

    def spread_v(h):
        for o in (2, 1, 3):
            cols = columns(lax.rem(x + o, n_head) * heads_here + h)
            to_head(1, h, o, v_hbm.at[:, :, cols], v_blk[h]).start()

    def arrived(kind, h, blocks):
        for o in range(1, n_head):
            pltpu.make_async_copy(
                blocks[h].at[mine], blocks[h].at[mine], a_recv.at[kind, h, o - 1]
            ).wait()

    def exchange(h):
        arrived(0, h, k_blk)
        arrived(1, h, v_blk)
        own_v[h].wait()

        @pl.loop(0, n_seq - 1)
        def _(d):
            peer = lax.rem(s + d + 1, n_seq)
            tile = wanted[peer]
            send[h, d, 0] = k_blk[h][tile]
            send[h, d, 1] = v_blk[h][tile]
            pltpu.make_async_remote_copy(
                src_ref=send.at[h, d],
                dst_ref=bank[h].at[s],
                send_sem=b_send.at[h],
                recv_sem=b_recv.at[h],
                device_id=(peer, x),
                device_id_type=MESH,
            ).start()

    q_scale = None
    for h in range(heads_here):
        spread(0, h, k_in, k_scale, gain_k, k_stage, k_blk)
        spread_v(h)
        bank[h][s] = jnp.zeros(bank[h].shape[1:], bank[h].dtype)
    load_q.wait()
    q_scale = row_scale(q_in, width) * (HD**-0.5 * LOG2E)
    for h in range(heads_here):
        spread(2, h, q_in, q_scale, gain_q, q_stage, q_blk)
    for h in range(heads_here):
        exchange(h)

    lane = lax.broadcasted_iota(jnp.int32, (1, TILE), 1)

    for h in range(heads_here):
        arrived(2, h, q_blk)
        landed = bank[h].at[pl.ds(0, n_seq - 1)]
        pltpu.make_async_copy(landed, landed, b_recv.at[h]).wait()

        @pl.loop(0, span_tiles)
        def _(step, h=h):
            o = n_head - 1 - step // own_tiles
            part = step % own_tiles
            dest = lax.rem(x + o, n_head)
            i = dest * own_tiles + part
            row = s * span_tiles + i
            count = counts[row]
            mate = i + 1 - 2 * (i % 2)
            keys, vals, bias = [], [], []
            for e in range(slots):
                g = listed[row, e]
                if e < 2:
                    own = i if e == 0 else mate
                    keys.append(k_blk[h][own])
                    vals.append(v_blk[h][own])
                else:
                    owner = g // span_tiles
                    keys.append(bank[h][owner, 0])
                    vals.append(bank[h][owner, 1])
                limit = jnp.where(e < count, valid[g], 0)
                bias.append(jnp.where(lane < limit, 0.0, MASKED))
            scores = lax.dot_general(
                q_blk[h][i], jnp.concatenate(keys, axis=0), (((1,), (1,)), ((), ())),
                preferred_element_type=jnp.float32,
            ) + jnp.concatenate(bias, axis=1)
            peak = jnp.max(scores, axis=1, keepdims=True)
            weights = jnp.exp2(scores - peak)
            total = jnp.sum(weights, axis=1, keepdims=True)
            mixed = jnp.dot(
                weights.astype(jnp.bfloat16), jnp.concatenate(vals, axis=0),
                preferred_element_type=jnp.float32,
            )
            out_stage[h, i] = (mixed / total).astype(jnp.bfloat16)

            @pl.when((part == own_tiles - 1) & (o > 0))
            def _():
                pltpu.make_async_remote_copy(
                    src_ref=out_stage.at[h, pl.ds(dest * own_tiles, own_tiles)],
                    dst_ref=o_hbm.at[:, :, columns(x * heads_here + h)],
                    send_sem=o_send.at[h],
                    recv_sem=o_recv.at[h],
                    device_id=(s, dest),
                    device_id_type=MESH,
                ).start()

        pltpu.make_async_copy(
            out_stage.at[h, mine], o_hbm.at[:, :, columns(x * heads_here + h)], o_own.at[h]
        ).start()

    for kind in range(3):
        pltpu.make_async_copy(k_stage, k_stage, a_send.at[kind]).wait()
    for h in range(heads_here):
        pltpu.make_async_copy(send.at[h], send.at[h], b_send.at[h]).wait()
        pltpu.make_async_copy(
            out_stage.at[h, mine], o_hbm.at[:, :, columns(x * heads_here + h)], o_own.at[h]
        ).wait()
        away = out_stage.at[h, pl.ds(0, span_tiles - own_tiles)]
        pltpu.make_async_copy(away, away, o_send.at[h]).wait()
        pltpu.make_async_copy(away, away, o_recv.at[h]).wait()


def on_device(queries, keys, values, gain_q, gain_k, key_tiles, tile_counts, tile_valid):
    n_head = lax.axis_size("head")
    n_seq = lax.axis_size("seq")
    rows, width = queries.shape
    own_tiles = rows // TILE
    span_tiles = own_tiles * n_head
    heads_here = width // HD // n_head
    slots = key_tiles.shape[1]
    s = lax.axis_index("seq")

    grid = key_tiles.reshape(n_seq, span_tiles, slots)
    used = lax.broadcasted_iota(jnp.int32, grid.shape, 2) < tile_counts.reshape(n_seq, span_tiles, 1)
    match = used & (grid // span_tiles == s)
    wanted = jnp.max(jnp.where(match, grid % span_tiles, 0), axis=(1, 2))

    smem = pl.BlockSpec(memory_space=pltpu.SMEM)
    vmem = pl.BlockSpec(memory_space=pltpu.VMEM)
    hbm = pl.BlockSpec(memory_space=pl.ANY)
    bf16 = jnp.bfloat16
    block = pltpu.VMEM((span_tiles, TILE, HD), bf16)
    stage = pltpu.VMEM((n_head - 1, heads_here, own_tiles, TILE, HD), bf16)
    shape = (own_tiles, TILE, width)
    dma = pltpu.SemaphoreType.DMA
    out = pl.pallas_call(
        functools.partial(kernel, n_seq, n_head, heads_here),
        out_shape=jax.ShapeDtypeStruct(shape, bf16),
        in_specs=[smem] * 4 + [hbm] * 3 + [vmem] * 2,
        out_specs=hbm,
        scratch_shapes=[
            pltpu.VMEM(shape, bf16),
            pltpu.VMEM(shape, bf16),
            stage,
            stage,
            pltpu.VMEM((heads_here, n_seq - 1, 2, TILE, HD), bf16),
            pltpu.VMEM((heads_here, span_tiles, TILE, HD), bf16),
            *[block] * (3 * heads_here),
            *[pltpu.VMEM((n_seq, 2, TILE, HD), bf16)] * heads_here,
            dma((2,)),
            dma((heads_here,)),
            dma((3,)),
            dma((3, heads_here, n_head - 1)),
            dma((heads_here,)),
            dma((heads_here,)),
            dma((heads_here,)),
            dma((heads_here,)),
            dma((heads_here,)),
        ],
        compiler_params=pltpu.CompilerParams(
            collective_id=0, has_side_effects=True, vmem_limit_bytes=56 << 20
        ),
    )(
        wanted, key_tiles, tile_counts, tile_valid,
        queries.reshape(shape), keys.reshape(shape), values.reshape(shape),
        gain_q.reshape(1, width), gain_k.reshape(1, width),
    )
    return out.reshape(rows, width)


def solution(mesh):
    placed = P(("seq", "head"), None)
    return jax.shard_map(
        on_device,
        mesh=mesh,
        in_specs=(placed, placed, placed, P(), P(), P(), P(), P()),
        out_specs=placed,
        check_vma=False,
    )
```

```python
import functools
import math

import jax
import jax.numpy as jnp
from jax import lax
from jax.experimental import pallas as pl
from jax.experimental.pallas import tpu as pltpu
from jax.sharding import PartitionSpec as P

HD = 128
TILE = 128
EPS = 1e-06
MASKED = -1e30
MESH = pl.DeviceIdType.MESH
LOG2E = math.log2(math.e)
SIDE = 4
CORES = 2
STRIDE = (SIDE * CORES, CORES)
HOPS = ((2, 0), (2, 1), (1, 0), (3, 0), (1, 1), (3, 1), (0, 1))
PIECE = 2


def schedule(heads):
    steps = [("spread", 0), ("spread", 1), ("scale_q", 0), ("ring", 0), ("spread_q", 0)]
    for t in range(1, heads + 3):
        steps += [("ring", t), ("spread", t + 1), ("relay", t - 1), ("pick", t - 1), ("spread_q", t), ("attend", t - 2)]
    return [(name, h) for name, h in steps if 0 <= h < heads]


def row_scale(rows_ref, width):
    groups = width // HD
    total = jnp.zeros((rows_ref.shape[0], TILE, HD), jnp.float32)
    for g in range(groups):
        part = rows_ref[:, :, g * HD : (g + 1) * HD].astype(jnp.float32)
        total = total + part * part
    return lax.rsqrt(jnp.sum(total, axis=-1, keepdims=True) / width + EPS)


def kernel(
    n_head, heads,
    wanted, listed, counts, valid, q_hbm, k_hbm, v_hbm, gain_q, gain_k,
    o_hbm,
    q_in, k_in, q_stage, k_stage, picked, out_stage, *rest,
):
    q_blk = rest[:heads]
    ring = (rest[heads : 2 * heads], rest[2 * heads : 3 * heads])
    bank = (rest[3 * heads : 4 * heads], rest[4 * heads : 5 * heads])
    (in_sem, own_sem, a_send, a_recv, r_send, r_recv, b_send, b_recv, o_send, o_recv, o_own) = rest[5 * heads :]
    s = lax.axis_index("seq")
    x = lax.axis_index("head")
    place = (s // STRIDE[0], s // STRIDE[1] % SIDE)
    core = s % CORES
    own_tiles = q_hbm.shape[0]
    span_tiles = own_tiles * n_head
    half = span_tiles // 2
    width = q_hbm.shape[2]
    slots = listed.shape[1]
    mine = pl.ds(x * own_tiles, own_tiles)
    states = {}

    def device(axis, along, cross, cores):
        moved = [place[0], place[1]]
        moved[axis] = lax.rem(place[axis] + along, SIDE)
        moved[1 - axis] = lax.rem(place[1 - axis] + cross, SIDE)
        return (moved[0] * STRIDE[0] + moved[1] * STRIDE[1] + lax.rem(core + cores, CORES), x)

    def columns(head):
        return pl.ds(pl.multiple_of(head * HD, HD), HD)

    load_k = pltpu.make_async_copy(k_hbm, k_in, in_sem.at[0])
    load_q = pltpu.make_async_copy(q_hbm, q_in, in_sem.at[1])
    load_k.start()
    load_q.start()

    def home(kind, h):
        return ring[kind][h].at[place[kind]] if kind < 2 else q_blk[h]

    own_v = []
    for h in range(heads):
        copy = pltpu.make_async_copy(
            v_hbm.at[:, :, columns(x * heads + h)], home(1, h).at[mine], own_sem.at[h]
        )
        copy.start()
        own_v.append(copy)

    barrier = pltpu.get_barrier_semaphore()
    friends = [(s, lax.rem(x + o, n_head)) for o in range(1, n_head)]
    friends += [device(0, 0, cross, cores) for cross, cores in HOPS]
    friends += [device(1, 0, cross, cores) for cross, cores in HOPS[:-1]]
    for friend in friends:
        pl.semaphore_signal(barrier, inc=1, device_id=friend, device_id_type=MESH)
    load_k.wait()
    states["k"] = row_scale(k_in, width)
    pl.semaphore_wait(barrier, len(friends))

    def to_head(kind, h, o, src):
        pltpu.make_async_remote_copy(
            src_ref=src,
            dst_ref=home(kind, h).at[mine],
            send_sem=a_send.at[kind],
            recv_sem=a_recv.at[kind, h, o - 1],
            device_id=(s, lax.rem(x + o, n_head)),
            device_id_type=MESH,
        ).start()

    def normalise(kind, h, rows_in, scale, gain, stage):
        for o in (2, 1, 3, 0):
            cols = columns(lax.rem(x + o, n_head) * heads + h)
            rows = rows_in[:, :, cols].astype(jnp.float32)
            rows = (rows * scale * gain[:, cols][None]).astype(jnp.bfloat16)
            if o == 0:
                home(kind, h)[mine] = rows
            else:
                stage[o - 1, h] = rows
                to_head(kind, h, o, stage.at[o - 1, h])

    def spread(h):
        normalise(0, h, k_in, states["k"], gain_k, k_stage)
        for o in (2, 1, 3):
            cols = columns(lax.rem(x + o, n_head) * heads + h)
            to_head(1, h, o, v_hbm.at[:, :, cols])

    def scale_q(h):
        load_q.wait()
        states["q"] = row_scale(q_in, width) * (HD**-0.5 * LOG2E)

    def spread_q(h):
        normalise(2, h, q_in, states["q"], gain_q, q_stage)

    def arrived(kind, h):
        for o in range(1, n_head):
            ref = home(kind, h).at[mine]
            pltpu.make_async_copy(ref, ref, a_recv.at[kind, h, o - 1]).wait()

    def ring_copy(kind, h, slot, tiles, along, sem):
        ref = ring[kind][h].at[slot, tiles]
        return pltpu.make_async_remote_copy(
            src_ref=ref,
            dst_ref=ref,
            send_sem=r_send.at[kind, h],
            recv_sem=r_recv.at[kind, h, sem],
            device_id=device(kind, along, 0, 0),
            device_id_type=MESH,
        )

    def ring_wait(kind, h, tiles, sem):
        ref = ring[kind][h].at[0, pl.ds(0, tiles)]
        pltpu.make_async_copy(ref, ref, r_recv.at[kind, h, sem]).wait()

    def ring_send(h):
        arrived(0, h)
        arrived(1, h)
        own_v[h].wait()
        for first in range(0, span_tiles, PIECE):
            for kind in (0, 1):
                for n, along in enumerate((1, SIDE - 1)):
                    ring_copy(kind, h, place[kind], pl.ds(first, PIECE), along, n).start()

    def relay(h):
        for kind in (0, 1):
            for n, along in enumerate((1, SIDE - 1)):
                ring_wait(kind, h, span_tiles, n)
        for first in range(0, half, PIECE):
            for kind in (0, 1):
                for n, along in enumerate((1, SIDE - 1)):
                    slot = lax.rem(place[kind] + SIDE - along, SIDE)
                    ring_copy(kind, h, slot, pl.ds(n * half + first, PIECE), along, 2 + n).start()

    def pick(h):
        for kind in (0, 1):
            for n in (0, 1):
                ring_wait(kind, h, half, 2 + n)
        for kind in (0, 1):
            here = place[1 - kind] * CORES + core
            for a in range(SIDE):
                bank[kind][h][here, a] = ring[kind][h][a, wanted[(kind * SIDE * CORES + here) * SIDE + a]]
        for n, (cross, cores) in enumerate(HOPS):
            for kind in (0, 1):
                row = lax.rem(place[1 - kind] + cross, SIDE) * CORES + lax.rem(core + cores, CORES)
                for a in range(SIDE):
                    tile = wanted[(kind * SIDE * CORES + row) * SIDE + a]
                    picked[kind, h, n, a] = ring[kind][h][a, tile]
                    if a % PIECE == PIECE - 1:
                        part = pl.ds(a + 1 - PIECE, PIECE)
                        pltpu.make_async_remote_copy(
                            src_ref=picked.at[kind, h, n, part],
                            dst_ref=bank[kind][h].at[place[1 - kind] * CORES + core, part],
                            send_sem=b_send.at[kind, h],
                            recv_sem=b_recv.at[kind, h],
                            device_id=device(kind, 0, cross, cores),
                            device_id_type=MESH,
                        ).start()

    lane = lax.broadcasted_iota(jnp.int32, (1, TILE), 1)

    def attend(h):
        arrived(2, h)
        for kind in (0, 1):
            landed = bank[kind][h].at[pl.ds(0, len(HOPS))]
            pltpu.make_async_copy(landed, landed, b_recv.at[kind, h]).wait()

        @pl.loop(0, span_tiles)
        def _(step):
            o = n_head - 1 - step // own_tiles
            part = step % own_tiles
            dest = lax.rem(x + o, n_head)
            i = dest * own_tiles + part
            row = s * span_tiles + i
            count = counts[row]
            mate = i + 1 - 2 * (i % 2)
            keys, vals, bias = [], [], []
            for e in range(slots):
                g = listed[row, e]
                if e < 2:
                    own = i if e == 0 else mate
                    keys.append(ring[0][h][place[0], own])
                    vals.append(ring[1][h][place[1], own])
                else:
                    owner = g // span_tiles
                    z, y, c = owner // STRIDE[0], owner // STRIDE[1] % SIDE, owner % CORES
                    keys.append(bank[0][h][y * CORES + c, z])
                    vals.append(bank[1][h][z * CORES + c, y])
                limit = jnp.where(e < count, valid[g], 0)
                bias.append(jnp.where(lane < limit, 0.0, MASKED))
            scores = lax.dot_general(
                q_blk[h][i], jnp.concatenate(keys, axis=0), (((1,), (1,)), ((), ())),
                preferred_element_type=jnp.float32,
            ) + jnp.concatenate(bias, axis=1)
            peak = jnp.max(scores, axis=1, keepdims=True)
            weights = jnp.exp2(scores - peak)
            total = jnp.sum(weights, axis=1, keepdims=True)
            mixed = jnp.dot(
                weights.astype(jnp.bfloat16), jnp.concatenate(vals, axis=0),
                preferred_element_type=jnp.float32,
            )
            out_stage[h, i] = (mixed / total).astype(jnp.bfloat16)

            @pl.when((part == own_tiles - 1) & (o > 0))
            def _():
                pltpu.make_async_remote_copy(
                    src_ref=out_stage.at[h, pl.ds(dest * own_tiles, own_tiles)],
                    dst_ref=o_hbm.at[:, :, columns(x * heads + h)],
                    send_sem=o_send.at[h],
                    recv_sem=o_recv.at[h],
                    device_id=(s, dest),
                    device_id_type=MESH,
                ).start()

        pltpu.make_async_copy(
            out_stage.at[h, mine], o_hbm.at[:, :, columns(x * heads + h)], o_own.at[h]
        ).start()

    stages = dict(
        spread=spread, scale_q=scale_q, spread_q=spread_q,
        ring=ring_send, relay=relay, pick=pick, attend=attend,
    )
    for name, h in schedule(heads):
        stages[name](h)

    for kind in range(3):
        pltpu.make_async_copy(k_stage, k_stage, a_send.at[kind]).wait()
    for h in range(heads):
        for kind in (0, 1):
            sent = ring[kind][h].at[pl.ds(0, 3)]
            pltpu.make_async_copy(sent, sent, r_send.at[kind, h]).wait()
            sent = picked.at[kind, h]
            pltpu.make_async_copy(sent, sent, b_send.at[kind, h]).wait()
        pltpu.make_async_copy(
            out_stage.at[h, mine], o_hbm.at[:, :, columns(x * heads + h)], o_own.at[h]
        ).wait()
        away = out_stage.at[h, pl.ds(0, span_tiles - own_tiles)]
        pltpu.make_async_copy(away, away, o_send.at[h]).wait()
        pltpu.make_async_copy(away, away, o_recv.at[h]).wait()


def wanted_tiles(grid, used, s):
    z, y, core = s // STRIDE[0], s // STRIDE[1] % SIDE, s % CORES
    slots = grid.shape[1] * grid.shape[2]
    tiles = jnp.where(used, grid, -1).reshape(SIDE, SIDE, CORES, slots)
    along_y = lax.dynamic_index_in_dim(tiles, z, 0, False).reshape(SIDE * CORES, 1, slots)
    along_z = lax.dynamic_index_in_dim(tiles, y, 1, False).reshape(SIDE * CORES, 1, slots)
    span = jnp.arange(SIDE, dtype=jnp.int32)[None, :, None]
    from_z = span * STRIDE[0] + y * STRIDE[1] + core
    from_y = z * STRIDE[0] + span * STRIDE[1] + core
    tile_count = grid.shape[1]
    found = [
        jnp.max(jnp.where((rows // tile_count == owner) & (rows >= 0), rows % tile_count, 0), axis=2)
        for rows, owner in ((along_y, from_z), (along_z, from_y))
    ]
    return jnp.stack(found).reshape(-1)


def on_device(queries, keys, values, gain_q, gain_k, key_tiles, tile_counts, tile_valid):
    n_head = lax.axis_size("head")
    n_seq = lax.axis_size("seq")
    rows, width = queries.shape
    own_tiles = rows // TILE
    span_tiles = own_tiles * n_head
    heads = width // HD // n_head
    slots = key_tiles.shape[1]
    s = lax.axis_index("seq")

    grid = key_tiles.reshape(n_seq, span_tiles, slots)
    used = lax.broadcasted_iota(jnp.int32, grid.shape, 2) < tile_counts.reshape(n_seq, span_tiles, 1)
    wanted = wanted_tiles(grid, used, s)

    smem = pl.BlockSpec(memory_space=pltpu.SMEM)
    vmem = pl.BlockSpec(memory_space=pltpu.VMEM)
    hbm = pl.BlockSpec(memory_space=pl.ANY)
    bf16 = jnp.bfloat16
    stage = pltpu.VMEM((n_head - 1, heads, own_tiles, TILE, HD), bf16)
    shape = (own_tiles, TILE, width)
    dma = pltpu.SemaphoreType.DMA
    out = pl.pallas_call(
        functools.partial(kernel, n_head, heads),
        out_shape=jax.ShapeDtypeStruct(shape, bf16),
        in_specs=[smem] * 4 + [hbm] * 3 + [vmem] * 2,
        out_specs=hbm,
        scratch_shapes=[
            pltpu.VMEM(shape, bf16),
            pltpu.VMEM(shape, bf16),
            stage,
            stage,
            pltpu.VMEM((2, heads, len(HOPS), SIDE, TILE, HD), bf16),
            pltpu.VMEM((heads, span_tiles, TILE, HD), bf16),
            *[pltpu.VMEM((span_tiles, TILE, HD), bf16)] * heads,
            *[pltpu.VMEM((SIDE, span_tiles, TILE, HD), bf16)] * (2 * heads),
            *[pltpu.VMEM((SIDE * CORES, SIDE, TILE, HD), bf16)] * (2 * heads),
            dma((2,)),
            dma((heads,)),
            dma((3,)),
            dma((3, heads, n_head - 1)),
            dma((2, heads)),
            dma((2, heads, 4)),
            dma((2, heads)),
            dma((2, heads)),
            dma((heads,)),
            dma((heads,)),
            dma((heads,)),
        ],
        compiler_params=pltpu.CompilerParams(
            collective_id=0, has_side_effects=True, vmem_limit_bytes=56 << 20
        ),
    )(
        wanted, key_tiles, tile_counts, tile_valid,
        queries.reshape(shape), keys.reshape(shape), values.reshape(shape),
        gain_q.reshape(1, width), gain_k.reshape(1, width),
    )
    return out.reshape(rows, width)


def solution(mesh):
    placed = P(("seq", "head"), None)
    return jax.shard_map(
        on_device,
        mesh=mesh,
        in_specs=(placed, placed, placed, P(), P(), P(), P(), P()),
        out_specs=placed,
        check_vma=False,
    )
```

```python
import functools
import math

import jax
import jax.numpy as jnp
from jax import lax
from jax.experimental import pallas as pl
from jax.experimental.pallas import tpu as pltpu
from jax.sharding import PartitionSpec as P

HD = 128
TILE = 128
EPS = 1e-06
MASKED = -1e30
MESH = pl.DeviceIdType.MESH
LOG2E = math.log2(math.e)
SIDE = 4
CORES = 2
STRIDE = (SIDE * CORES, CORES)
HOPS = ((2, 0), (2, 1), (1, 0), (3, 0), (1, 1), (3, 1), (0, 1))
EARLY = 4


def schedule(heads):
    steps = [("send_v", 0), ("ring_own_v", 0), ("send_k", 0), ("ring_own_k", 0)]
    for h in range(1, heads):
        steps += [("ring_own_v", h), ("ring_own_k", h)]
    steps += [("spread", 1), ("scale_q", 0), ("spread_q", 0), ("spread", 2)]
    steps += [("ring_rest", 0), ("ring_rest", 1), ("relay", 0)]
    for t in range(heads + 1):
        steps += [("pick_first", t), ("relay", t + 1), ("pick_last", t), ("ring_rest", t + 2)]
        steps += [("spread", t + 3), ("spread_q", t + 1), ("attend", t - 1)]
    return [(name, h) for name, h in steps if 0 <= h < heads]


def row_scale(rows_ref, width):
    groups = width // HD
    total = jnp.zeros((rows_ref.shape[0], TILE, HD), jnp.float32)
    for g in range(groups):
        part = rows_ref[:, :, g * HD : (g + 1) * HD].astype(jnp.float32)
        total = total + part * part
    return lax.rsqrt(jnp.sum(total, axis=-1, keepdims=True) / width + EPS)


def find_wanted(s, place, core, span_tiles, listed_rows, count_row, found):
    slots, tiles = listed_rows.shape
    used = lax.broadcasted_iota(jnp.int32, (slots, tiles), 0) < count_row[...][None]
    listed = jnp.where(used, listed_rows[...], -1)
    owner = listed >> (span_tiles.bit_length() - 1)
    tile = listed & (span_tiles - 1)
    for kind in (0, 1):
        for a in range(SIDE):
            source = s + (a - place[kind]) * STRIDE[kind]
            best = jnp.max(jnp.where(owner == source, tile, 0), axis=0, keepdims=True)
            found[pl.ds(kind * SIDE + a, 1), :] = best
    best = found[...]
    for step in (1, 2, 4):
        best = jnp.maximum(best, pltpu.roll(best, tiles - step, 1))
    found[...] = best


def kernel(
    n_head, heads,
    listed, counts, valid, q_hbm, k_hbm, v_hbm, gain_q, gain_k, listed_rows, count_row,
    o_hbm,
    q_in, k_in, q_stage, k_stage, picked, out_stage, found, wanted, *rest,
):
    q_blk = rest[:heads]
    ring = (rest[heads : 2 * heads], rest[2 * heads : 3 * heads])
    bank = (rest[3 * heads : 4 * heads], rest[4 * heads : 5 * heads])
    (in_sem, own_sem, a_send, a_recv, r_send, r_recv, b_send, b_recv, o_send, o_recv, o_own) = rest[5 * heads :]
    s = lax.axis_index("seq")
    x = lax.axis_index("head")
    place = (s // STRIDE[0], s // STRIDE[1] % SIDE)
    core = s % CORES
    own_tiles = q_hbm.shape[0]
    span_tiles = own_tiles * n_head
    half = span_tiles // 2
    width = q_hbm.shape[2]
    slots = listed.shape[0]
    mine = pl.ds(x * own_tiles, own_tiles)
    states = {}

    def device(axis, along, cross, cores):
        moved = [place[0], place[1]]
        moved[axis] = lax.rem(place[axis] + along, SIDE)
        moved[1 - axis] = lax.rem(place[1 - axis] + cross, SIDE)
        return (moved[0] * STRIDE[0] + moved[1] * STRIDE[1] + lax.rem(core + cores, CORES), x)

    def columns(head):
        return pl.ds(pl.multiple_of(head * HD, HD), HD)

    load_k = pltpu.make_async_copy(k_hbm, k_in, in_sem.at[0])
    load_q = pltpu.make_async_copy(q_hbm, q_in, in_sem.at[1])
    load_k.start()
    load_q.start()

    def home(kind, h):
        return ring[kind][h].at[place[kind]] if kind < 2 else q_blk[h]

    own_v = []
    for h in range(heads):
        copy = pltpu.make_async_copy(
            v_hbm.at[:, :, columns(x * heads + h)], home(1, h).at[mine], own_sem.at[h]
        )
        copy.start()
        own_v.append(copy)

    barrier = pltpu.get_barrier_semaphore()
    friends = [(s, lax.rem(x + o, n_head)) for o in range(1, n_head)]
    friends += [device(0, 0, cross, cores) for cross, cores in HOPS]
    friends += [device(1, 0, cross, cores) for cross, cores in HOPS[:-1]]
    for friend in friends:
        pl.semaphore_signal(barrier, inc=1, device_id=friend, device_id_type=MESH)
    find_wanted(s, place, core, span_tiles, listed_rows, count_row, found)
    to_smem = pltpu.make_async_copy(found, wanted, in_sem.at[2])
    to_smem.start()
    load_k.wait()
    states["k"] = row_scale(k_in, width)
    to_smem.wait()
    pl.semaphore_wait(barrier, len(friends))

    def to_head(kind, h, o, src):
        pltpu.make_async_remote_copy(
            src_ref=src,
            dst_ref=home(kind, h).at[mine],
            send_sem=a_send.at[kind],
            recv_sem=a_recv.at[kind, h, o - 1],
            device_id=(s, lax.rem(x + o, n_head)),
            device_id_type=MESH,
        ).start()

    def normalised(rows_in, scale, gain, head):
        cols = columns(head)
        return (rows_in[:, :, cols].astype(jnp.float32) * scale * gain[cols][None, None]).astype(jnp.bfloat16)

    def send_normalised(kind, h, rows_in, scale, gain, stage):
        for o in (2, 1, 3):
            stage[o - 1, h] = normalised(rows_in, scale, gain, lax.rem(x + o, n_head) * heads + h)
            to_head(kind, h, o, stage.at[o - 1, h])

    def send_k(h):
        send_normalised(0, h, k_in, states["k"], gain_k, k_stage)

    def send_v(h):
        for o in (2, 1, 3):
            cols = columns(lax.rem(x + o, n_head) * heads + h)
            to_head(1, h, o, v_hbm.at[:, :, cols])

    def spread(h):
        send_v(h)
        send_k(h)

    def ring_own_k(h):
        home(0, h)[mine] = normalised(k_in, states["k"], gain_k, x * heads + h)
        ring_piece(0, h, 0)

    def ring_own_v(h):
        own_v[h].wait()
        ring_piece(1, h, 0)

    def scale_q(h):
        load_q.wait()
        states["q"] = row_scale(q_in, width) * (HD**-0.5 * LOG2E)

    def spread_q(h):
        q_blk[h][mine] = normalised(q_in, states["q"], gain_q, x * heads + h)
        send_normalised(2, h, q_in, states["q"], gain_q, q_stage)

    def arrived(kind, h, o):
        ref = home(kind, h).at[mine]
        pltpu.make_async_copy(ref, ref, a_recv.at[kind, h, o - 1]).wait()

    def ring_copy(kind, h, slot, tiles, along, sem):
        ref = ring[kind][h].at[slot, tiles]
        return pltpu.make_async_remote_copy(
            src_ref=ref,
            dst_ref=ref,
            send_sem=r_send.at[kind, h],
            recv_sem=r_recv.at[kind, h, sem],
            device_id=device(kind, along, 0, 0),
            device_id_type=MESH,
        )

    def ring_wait(kind, h, tiles, sem):
        ref = ring[kind][h].at[0, pl.ds(0, tiles)]
        pltpu.make_async_copy(ref, ref, r_recv.at[kind, h, sem]).wait()

    def ring_piece(kind, h, o):
        tiles = pl.ds(lax.rem(x + n_head - o, n_head) * own_tiles, own_tiles)
        for n, along in enumerate((1, SIDE - 1)):
            ring_copy(kind, h, place[kind], tiles, along, n).start()

    def ring_rest(h):
        for o in (1, 3, 2):
            for kind in (1, 0):
                arrived(kind, h, o)
                ring_piece(kind, h, o)

    def relay(h):
        for kind in (0, 1):
            for n, along in enumerate((1, SIDE - 1)):
                ring_wait(kind, h, span_tiles, n)
        for kind in (0, 1):
            for n, along in enumerate((1, SIDE - 1)):
                slot = lax.rem(place[kind] + SIDE - along, SIDE)
                ring_copy(kind, h, slot, pl.ds(n * half, half), along, 2 + n).start()

    def pick(h, hops):
        for n in hops:
            cross, cores = HOPS[n]
            for kind in (0, 1):
                dest = device(kind, 0, cross, cores)
                for a in range(SIDE):
                    picked[kind, h, n, a] = ring[kind][h][a, wanted[kind * SIDE + a, dest[0] * span_tiles]]
                pltpu.make_async_remote_copy(
                    src_ref=picked.at[kind, h, n],
                    dst_ref=bank[kind][h].at[place[1 - kind] * CORES + core],
                    send_sem=b_send.at[kind, h],
                    recv_sem=b_recv.at[kind, h],
                    device_id=dest,
                    device_id_type=MESH,
                ).start()

    def pick_first(h):
        for kind in (0, 1):
            for n in (0, 1):
                ring_wait(kind, h, half, 2 + n)
        pick(h, range(0, EARLY))

    def pick_last(h):
        pick(h, range(EARLY, len(HOPS)))
        for kind in (0, 1):
            for a in range(SIDE):
                bank[kind][h][place[1 - kind] * CORES + core, a] = ring[kind][h][
                    a, wanted[kind * SIDE + a, s * span_tiles]
                ]

    lane = lax.broadcasted_iota(jnp.int32, (1, TILE), 1)

    def attend(h):
        for o in range(1, n_head):
            arrived(2, h, o)
        for kind in (0, 1):
            landed = bank[kind][h].at[pl.ds(0, len(HOPS))]
            pltpu.make_async_copy(landed, landed, b_recv.at[kind, h]).wait()

        @pl.loop(0, span_tiles)
        def _(step):
            o = n_head - 1 - step // own_tiles
            part = step % own_tiles
            dest = lax.rem(x + o, n_head)
            i = dest * own_tiles + part
            row = s * span_tiles + i
            count = counts[row]
            mate = i + 1 - 2 * (i % 2)
            keys, vals, bias = [], [], []
            for e in range(slots):
                g = listed[e, row]
                if e < 2:
                    own = i if e == 0 else mate
                    keys.append(ring[0][h][place[0], own])
                    vals.append(ring[1][h][place[1], own])
                else:
                    owner = g // span_tiles
                    z, y, c = owner // STRIDE[0], owner // STRIDE[1] % SIDE, owner % CORES
                    keys.append(bank[0][h][y * CORES + c, z])
                    vals.append(bank[1][h][z * CORES + c, y])
                limit = jnp.where(e < count, valid[g], 0)
                bias.append(jnp.where(lane < limit, 0.0, MASKED))
            scores = lax.dot_general(
                q_blk[h][i], jnp.concatenate(keys, axis=0), (((1,), (1,)), ((), ())),
                preferred_element_type=jnp.float32,
            ) + jnp.concatenate(bias, axis=1)
            peak = jnp.max(scores, axis=1, keepdims=True)
            weights = jnp.exp2(scores - peak)
            total = jnp.sum(weights, axis=1, keepdims=True)
            mixed = jnp.dot(
                weights.astype(jnp.bfloat16), jnp.concatenate(vals, axis=0),
                preferred_element_type=jnp.float32,
            )
            out_stage[h, i] = (mixed / total).astype(jnp.bfloat16)

            @pl.when((part == own_tiles - 1) & (o > 0))
            def _():
                pltpu.make_async_remote_copy(
                    src_ref=out_stage.at[h, pl.ds(dest * own_tiles, own_tiles)],
                    dst_ref=o_hbm.at[:, :, columns(x * heads + h)],
                    send_sem=o_send.at[h],
                    recv_sem=o_recv.at[h],
                    device_id=(s, dest),
                    device_id_type=MESH,
                ).start()

        pltpu.make_async_copy(
            out_stage.at[h, mine], o_hbm.at[:, :, columns(x * heads + h)], o_own.at[h]
        ).start()

    stages = dict(
        send_v=send_v, send_k=send_k, spread=spread, scale_q=scale_q, spread_q=spread_q,
        ring_own_k=ring_own_k, ring_own_v=ring_own_v, ring_rest=ring_rest,
        relay=relay, pick_first=pick_first, pick_last=pick_last, attend=attend,
    )
    for name, h in schedule(heads):
        stages[name](h)

    for kind in range(3):
        pltpu.make_async_copy(k_stage, k_stage, a_send.at[kind]).wait()
    for h in range(heads):
        for kind in (0, 1):
            sent = ring[kind][h].at[pl.ds(0, 3)]
            pltpu.make_async_copy(sent, sent, r_send.at[kind, h]).wait()
            sent = picked.at[kind, h]
            pltpu.make_async_copy(sent, sent, b_send.at[kind, h]).wait()
        pltpu.make_async_copy(
            out_stage.at[h, mine], o_hbm.at[:, :, columns(x * heads + h)], o_own.at[h]
        ).wait()
        away = out_stage.at[h, pl.ds(0, span_tiles - own_tiles)]
        pltpu.make_async_copy(away, away, o_send.at[h]).wait()
        pltpu.make_async_copy(away, away, o_recv.at[h]).wait()


def on_device(queries, keys, values, gain_q, gain_k, key_tiles, tile_counts, tile_valid):
    n_head = lax.axis_size("head")
    rows, width = queries.shape
    own_tiles = rows // TILE
    span_tiles = own_tiles * n_head
    heads = width // HD // n_head
    tiles = key_tiles.shape[0]
    listed = key_tiles.T
    smem = pl.BlockSpec(memory_space=pltpu.SMEM)
    vmem = pl.BlockSpec(memory_space=pltpu.VMEM)
    hbm = pl.BlockSpec(memory_space=pl.ANY)
    bf16 = jnp.bfloat16
    stage = pltpu.VMEM((n_head - 1, heads, own_tiles, TILE, HD), bf16)
    shape = (own_tiles, TILE, width)
    dma = pltpu.SemaphoreType.DMA
    out = pl.pallas_call(
        functools.partial(kernel, n_head, heads),
        out_shape=jax.ShapeDtypeStruct(shape, bf16),
        in_specs=[smem] * 3 + [hbm] * 3 + [vmem] * 4,
        out_specs=hbm,
        scratch_shapes=[
            pltpu.VMEM(shape, bf16),
            pltpu.VMEM(shape, bf16),
            stage,
            stage,
            pltpu.VMEM((2, heads, len(HOPS), SIDE, TILE, HD), bf16),
            pltpu.VMEM((heads, span_tiles, TILE, HD), bf16),
            pltpu.VMEM((2 * SIDE, tiles), jnp.int32),
            pltpu.SMEM((2 * SIDE, tiles), jnp.int32),
            *[pltpu.VMEM((span_tiles, TILE, HD), bf16)] * heads,
            *[pltpu.VMEM((SIDE, span_tiles, TILE, HD), bf16)] * (2 * heads),
            *[pltpu.VMEM((SIDE * CORES, SIDE, TILE, HD), bf16)] * (2 * heads),
            dma((3,)),
            dma((heads,)),
            dma((3,)),
            dma((3, heads, n_head - 1)),
            dma((2, heads)),
            dma((2, heads, 4)),
            dma((2, heads)),
            dma((2, heads)),
            dma((heads,)),
            dma((heads,)),
            dma((heads,)),
        ],
        compiler_params=pltpu.CompilerParams(
            collective_id=0, has_side_effects=True, vmem_limit_bytes=56 << 20
        ),
    )(
        listed, tile_counts, tile_valid,
        queries.reshape(shape), keys.reshape(shape), values.reshape(shape),
        gain_q, gain_k, listed, tile_counts,
    )
    return out.reshape(rows, width)


def solution(mesh):
    placed = P(("seq", "head"), None)
    return jax.shard_map(
        on_device,
        mesh=mesh,
        in_specs=(placed, placed, placed, P(), P(), P(), P(), P()),
        out_specs=placed,
        check_vma=False,
    )
```

```python
import functools
import math

import jax
import jax.numpy as jnp
from jax import lax
from jax.experimental import pallas as pl
from jax.experimental.pallas import tpu as pltpu
from jax.sharding import PartitionSpec as P

HD = 128
TILE = 128
EPS = 1e-06
MASKED = -1e30
MESH = pl.DeviceIdType.MESH
LOG2E = math.log2(math.e)
SIDE = 4
CORES = 2
STRIDE = (SIDE * CORES, CORES)
COLUMNS = SIDE * SIDE
HOPS = ((2, 0), (2, 1), (1, 0), (3, 0), (1, 1), (3, 1), (0, 1))
CHUNKS = (0, 1, 3, 2)
GROUPS = 4
K, V, Q = 0, 1, 2


def schedule():
    return (
        [("send", V), ("scale", K), ("spread_k", 0), ("send", K)]
        + [("own_ring", V), ("own_ring", K), ("direct", K, 0), ("spread_v", 0)]
        + [("direct", K, q) for q in CHUNKS[1:]]
        + [("scale", Q), ("spread_q", 0), ("send", Q)]
        + [("pass_on", K, 0), ("ring_rest", 0), ("direct", V, 0), ("pass_on", K, 1), ("pass_on", K, 3)]
        + [("direct", V, 1), ("pass_on", K, 2), ("finish", K, 0), ("direct", V, 3), ("finish", K, 1)]
        + [("relay", 0), ("direct", V, 2), ("finish", K, 3), ("finish", K, 2), ("pick", 0)]
        + [("complete", K), ("weigh", 0), ("pass_on", V, 0), ("weigh", 1), ("pass_on", V, 1)]
        + [("finish", V, 0), ("attend", 0), ("pass_on", V, 3), ("weigh", 2), ("pass_on", V, 2)]
        + [("finish", V, 1), ("weigh", 3), ("finish", V, 3), ("finish", V, 2)]
        + [("complete", V), ("mix", 0)]
    )


def row_scale(rows_ref, width):
    total = jnp.zeros((rows_ref.shape[0], TILE, HD), jnp.float32)
    for g in range(width // HD):
        part = rows_ref[:, :, g * HD : (g + 1) * HD].astype(jnp.float32)
        total = total + part * part
    return lax.rsqrt(jnp.sum(total, axis=-1, keepdims=True) / width + EPS)


def find_wanted(s, place, span_tiles, listed_rows, count_row, found):
    slots, tiles = listed_rows.shape
    used = lax.broadcasted_iota(jnp.int32, (slots, tiles), 0) < count_row[...][None]
    listed = jnp.where(used, listed_rows[...], -1)
    owner = listed >> (span_tiles.bit_length() - 1)
    tile = listed & (span_tiles - 1)
    for kind in (K, V):
        for a in range(SIDE):
            source = s + (a - place[kind]) * STRIDE[kind]
            best = jnp.max(jnp.where(owner == source, tile, 0), axis=0, keepdims=True)
            found[pl.ds(kind * SIDE + a, 1), :] = best
    best = found[...]
    for step in (1, 2, 4):
        best = jnp.maximum(best, pltpu.roll(best, tiles - step, 1))
    found[...] = best


def kernel(
    n_head,
    listed, counts, valid, q_hbm, k_hbm, v_hbm, gain_q, gain_k, listed_rows, count_row,
    o_ref,
    q_in, k_in, q_norm, k_norm, found, wanted,
    col_k, col_v, col_q, col_out, weights, inverse,
    ring_k, ring_v, bank_k, bank_v, blk_q, picked, blk_out,
    in_sem, own_sem, m_send, m_recv, x_send, x_recv, c_send, c_recv,
    a_send, a_recv, r_send, r_recv, b_send, b_recv, o_send, o_recv, o_own,
):
    s = lax.axis_index("seq")
    x = lax.axis_index("head")
    place = (s // STRIDE[0], s // STRIDE[1] % SIDE)
    core = s % CORES
    here = place[0] * SIDE + place[1]
    own_tiles = q_hbm.shape[0]
    span_tiles = own_tiles * n_head
    half = span_tiles // 2
    width = q_hbm.shape[2]
    slots = listed.shape[0]
    mine = pl.ds(x * own_tiles, own_tiles)
    raw = (k_in, None, q_in)
    norm = (k_norm, None, q_norm)
    gain = (gain_k, None, gain_q)
    col = (col_k, col_v, col_q)
    ring = (ring_k, ring_v)
    bank = (bank_k, bank_v)
    scales = {}

    def device(dz, dy, cores):
        z = lax.rem(place[0] + dz, SIDE)
        y = lax.rem(place[1] + dy, SIDE)
        return (z * STRIDE[0] + y * STRIDE[1] + lax.rem(core + cores, CORES), x)

    def crossing(kind, along, cross, cores):
        return device(along, cross, cores) if kind == K else device(cross, along, cores)

    def beside(o):
        return (s, lax.rem(x + o, n_head))

    def columns(head):
        return pl.ds(pl.multiple_of(head * HD, HD), HD)

    def remote(src, dst, send_sem, recv_sem, dest):
        pltpu.make_async_remote_copy(
            src_ref=src, dst_ref=dst, send_sem=send_sem, recv_sem=recv_sem,
            device_id=dest, device_id_type=MESH,
        ).start()

    def await_bytes(ref, sem):
        pltpu.make_async_copy(ref, ref, sem).wait()

    load_k = pltpu.make_async_copy(k_hbm, k_in, in_sem.at[0])
    load_q = pltpu.make_async_copy(q_hbm, q_in, in_sem.at[1])
    load_k.start()
    load_q.start()
    rest_head = COLUMNS + x
    own_rest = pltpu.make_async_copy(
        v_hbm.at[:, :, columns(rest_head)], ring_v.at[place[1], mine], own_sem.at[0]
    )
    own_col = pltpu.make_async_copy(
        v_hbm.at[:, :, columns(here)], col_v.at[core, x, here], own_sem.at[1]
    )
    own_rest.start()
    own_col.start()

    barrier = pltpu.get_barrier_semaphore()
    friends = [beside(o) for o in range(1, n_head)]
    friends += [device(dz, dy, 0) for dz in range(SIDE) for dy in range(SIDE) if dz + dy]
    friends += [device(0, dy, 1) for dy in range(SIDE)] + [device(dz, 0, 1) for dz in range(1, SIDE)]
    for friend in friends:
        pl.semaphore_signal(barrier, inc=1, device_id=friend, device_id_type=MESH)
    find_wanted(s, place, span_tiles, listed_rows, count_row, found)
    to_smem = pltpu.make_async_copy(found, wanted, in_sem.at[2])
    to_smem.start()
    pl.semaphore_wait(barrier, len(friends))

    def scale(kind):
        (load_k if kind == K else load_q).wait()
        scales[kind] = row_scale(raw[kind], width)
        if kind == Q:
            scales[kind] = scales[kind] * (HD**-0.5 * LOG2E)

    def normalised(kind, head):
        cols = columns(head)
        rows = raw[kind][:, :, cols].astype(jnp.float32)
        return (rows * scales[kind] * gain[kind][cols][None, None]).astype(jnp.bfloat16)

    def source(kind, head):
        if kind == V:
            return v_hbm.at[:, :, columns(head)]
        norm[kind][head] = normalised(kind, head)
        return norm[kind].at[head]

    def to_columns(kind):
        for dz in CHUNKS:
            for dy in CHUNKS:
                if dz + dy:
                    z, y = lax.rem(place[0] + dz, SIDE), lax.rem(place[1] + dy, SIDE)
                    landing = col_q.at[here] if kind == Q else col[kind].at[core, x, here]
                    remote(
                        source(kind, z * SIDE + y), landing, m_send.at[kind],
                        m_recv.at[kind, (SIDE - dz) % SIDE], device(dz, dy, 0),
                    )

    def spread_k(_):
        col_k[core, x, here] = normalised(K, here)
        to_columns(K)

    def spread_v(_):
        to_columns(V)

    def spread_q(_):
        col_q[here] = normalised(Q, here)
        to_columns(Q)

    def chunk_rows(q, first=0, count=SIDE):
        return pl.ds(lax.rem(place[0] + q, SIDE) * SIDE + first, count)

    def chunk_wait(kind, q):
        landed = col_k.at[0, 0, pl.ds(0, SIDE - 1 if q == 0 else SIDE)]
        await_bytes(landed, m_recv.at[kind, q])

    def across(kind, slot, rows):
        ref = col[kind].at[core, slot, rows]
        remote(ref, ref, c_send.at[kind], c_recv.at[kind], device(0, 0, 1))

    def direct(kind, q):
        if kind == V and q == 0:
            own_col.wait()
        chunk_wait(kind, q)
        ref = col[kind].at[core, x, chunk_rows(q)]
        for n, along in enumerate((1, SIDE - 1)):
            remote(ref, ref, x_send.at[kind], x_recv.at[kind, n, q], beside(along))
        across(kind, x, chunk_rows(q))

    def pass_on(kind, q):
        for n, along in enumerate((1, SIDE - 1)):
            slot = lax.rem(x + SIDE - along, SIDE)
            await_bytes(col[kind].at[core, slot, chunk_rows(q)], x_recv.at[kind, n, q])
            ref = col[kind].at[core, slot, chunk_rows(q, n * (SIDE // 2), SIDE // 2)]
            remote(ref, ref, x_send.at[kind], x_recv.at[kind, 2 + n, q], beside(along))
            across(kind, slot, chunk_rows(q))

    def finish(kind, q):
        slot = lax.rem(x + SIDE // 2, SIDE)
        for n in (0, 1):
            ref = col[kind].at[core, slot, chunk_rows(q, n * (SIDE // 2), SIDE // 2)]
            await_bytes(ref, x_recv.at[kind, 2 + n, q])
        across(kind, slot, chunk_rows(q))

    def complete(kind):
        await_bytes(col[kind].at[1 - core], c_recv.at[kind])
        if kind == K:
            for q in CHUNKS:
                chunk_wait(Q, q)

    lane = lax.broadcasted_iota(jnp.int32, (1, TILE), 1)

    def key_bias(row):
        count = counts[row]
        bias = []
        for e in range(slots):
            limit = jnp.where(e < count, valid[listed[e, row]], 0)
            bias.append(jnp.where(lane < limit, 0.0, MASKED))
        return jnp.concatenate(bias, axis=1)

    def softmax(query, keys, bias):
        scores = lax.dot_general(
            query, jnp.concatenate(keys, axis=0), (((1,), (1,)), ((), ())),
            preferred_element_type=jnp.float32,
        ) + bias
        rows = jnp.exp2(scores - jnp.max(scores, axis=1, keepdims=True))
        return rows.astype(jnp.bfloat16), 1.0 / jnp.sum(rows, axis=1, keepdims=True)

    def col_tile(ref, g):
        block = g // span_tiles
        return ref[block % CORES, g % span_tiles // own_tiles, block // CORES, g % own_tiles]

    def col_row(block, part):
        return (block * CORES + core) * span_tiles + x * own_tiles + part

    def weigh(group):
        each = COLUMNS // GROUPS

        @pl.loop(group * each, (group + 1) * each)
        def _(block):
            for part in range(own_tiles):
                row = col_row(block, part)
                keys = [col_tile(col_k, listed[e, row]) for e in range(slots)]
                rows, inv = softmax(col_q[block, part], keys, key_bias(row))
                weights[block, part] = rows
                inverse[block, part] = inv

    def mix(_):
        @pl.loop(0, COLUMNS)
        def _(step):
            off = COLUMNS - 1 - step
            dz, dy = off // SIDE, off % SIDE
            z, y = lax.rem(place[0] + dz, SIDE), lax.rem(place[1] + dy, SIDE)
            block = z * SIDE + y
            for part in range(own_tiles):
                row = col_row(block, part)
                vals = [col_tile(col_v, listed[e, row]) for e in range(slots)]
                mixed = jnp.dot(
                    weights[block, part], jnp.concatenate(vals, axis=0),
                    preferred_element_type=jnp.float32,
                )
                col_out[block, part] = (mixed * inverse[block, part]).astype(jnp.bfloat16)

            @pl.when(off > 0)
            def _():
                remote(
                    col_out.at[block], o_ref.at[:, :, columns(here)], o_send.at[0], o_recv.at[0],
                    (z * STRIDE[0] + y * STRIDE[1] + core, x),
                )

        pltpu.make_async_copy(col_out.at[here], o_ref.at[:, :, columns(here)], o_own.at[0]).start()

    def home(kind):
        return blk_q if kind == Q else ring[kind].at[place[kind]]

    def send(kind):
        for o in (2, 1, 3):
            remote(
                source(kind, COLUMNS + lax.rem(x + o, n_head)), home(kind).at[mine],
                a_send.at[kind], a_recv.at[kind, o - 1], beside(o),
            )
        if kind == Q:
            blk_q[mine] = normalised(Q, rest_head)

    def arrived(kind, o):
        await_bytes(home(kind).at[mine], a_recv.at[kind, o - 1])

    def ring_copy(kind, slot, tiles, n, sem):
        ref = ring[kind].at[slot, tiles]
        along = (1, SIDE - 1)[n]
        remote(ref, ref, r_send.at[kind], r_recv.at[kind, sem], crossing(kind, along, 0, 0))

    def ring_piece(kind, o):
        tiles = pl.ds(lax.rem(x + n_head - o, n_head) * own_tiles, own_tiles)
        for n in (0, 1):
            ring_copy(kind, place[kind], tiles, n, n)

    def own_ring(kind):
        if kind == V:
            own_rest.wait()
        else:
            ring_k[place[K], mine] = normalised(K, rest_head)
        ring_piece(kind, 0)

    def ring_rest(_):
        for o in (1, 3, 2):
            for kind in (V, K):
                arrived(kind, o)
                ring_piece(kind, o)

    def relay(_):
        for kind in (K, V):
            for n in (0, 1):
                await_bytes(ring[kind].at[0], r_recv.at[kind, n])
        for kind in (K, V):
            for n, along in enumerate((1, SIDE - 1)):
                slot = lax.rem(place[kind] + SIDE - along, SIDE)
                ring_copy(kind, slot, pl.ds(n * half, half), n, 2 + n)

    def pick(_):
        to_smem.wait()
        for kind in (K, V):
            for n in (0, 1):
                await_bytes(ring[kind].at[0, pl.ds(0, half)], r_recv.at[kind, 2 + n])
        for n, (cross, cores) in enumerate(HOPS):
            for kind in (K, V):
                dest = crossing(kind, 0, cross, cores)
                for a in range(SIDE):
                    picked[kind, n, a] = ring[kind][a, wanted[kind * SIDE + a, dest[0] * span_tiles]]
                remote(
                    picked.at[kind, n], bank[kind].at[place[1 - kind] * CORES + core],
                    b_send.at[kind], b_recv.at[kind], dest,
                )
        for kind in (K, V):
            for a in range(SIDE):
                bank[kind][place[1 - kind] * CORES + core, a] = ring[kind][
                    a, wanted[kind * SIDE + a, s * span_tiles]
                ]

    def attend(_):
        for o in range(1, n_head):
            arrived(Q, o)
        for kind in (K, V):
            await_bytes(bank[kind].at[pl.ds(0, len(HOPS))], b_recv.at[kind])

        @pl.loop(0, span_tiles)
        def _(step):
            o = n_head - 1 - step // own_tiles
            part = step % own_tiles
            dest = lax.rem(x + o, n_head)
            i = dest * own_tiles + part
            row = s * span_tiles + i
            mate = i + 1 - 2 * (i % 2)
            keys = [ring_k[place[K], i], ring_k[place[K], mate]]
            vals = [ring_v[place[V], i], ring_v[place[V], mate]]
            for e in range(2, slots):
                owner = listed[e, row] // span_tiles
                z, y, c = owner // STRIDE[0], owner // STRIDE[1] % SIDE, owner % CORES
                keys.append(bank_k[y * CORES + c, z])
                vals.append(bank_v[z * CORES + c, y])
            rows, inv = softmax(blk_q[i], keys, key_bias(row))
            mixed = jnp.dot(rows, jnp.concatenate(vals, axis=0), preferred_element_type=jnp.float32)
            blk_out[i] = (mixed * inv).astype(jnp.bfloat16)

            @pl.when((part == own_tiles - 1) & (o > 0))
            def _():
                remote(
                    blk_out.at[pl.ds(dest * own_tiles, own_tiles)], o_ref.at[:, :, columns(rest_head)],
                    o_send.at[1], o_recv.at[1], (s, dest),
                )

        pltpu.make_async_copy(blk_out.at[mine], o_ref.at[:, :, columns(rest_head)], o_own.at[1]).start()

    stages = dict(
        send=send, scale=scale, spread_k=spread_k, spread_v=spread_v, spread_q=spread_q,
        own_ring=own_ring, direct=direct, pass_on=pass_on, finish=finish, complete=complete,
        ring_rest=ring_rest, relay=relay, pick=pick, weigh=weigh, attend=attend, mix=mix,
    )
    for name, *args in schedule():
        stages[name](*args)

    away = col_q.at[pl.ds(0, COLUMNS - 1)]
    aside = blk_q.at[pl.ds(0, span_tiles - own_tiles)]
    for kind in (K, V, Q):
        await_bytes(away, m_send.at[kind])
        await_bytes(aside, a_send.at[kind])
    for kind in (K, V):
        await_bytes(col_k.at[0, pl.ds(0, 3)], x_send.at[kind])
        await_bytes(col_k.at[0], c_send.at[kind])
        await_bytes(ring_k.at[pl.ds(0, 3)], r_send.at[kind])
        await_bytes(picked.at[kind], b_send.at[kind])
    for n, (moved, kept, head) in enumerate(
        ((away, col_out.at[here], here), (aside, blk_out.at[mine], rest_head))
    ):
        await_bytes(moved, o_send.at[n])
        await_bytes(moved, o_recv.at[n])
        pltpu.make_async_copy(kept, o_ref.at[:, :, columns(head)], o_own.at[n]).wait()


def on_device(queries, keys, values, gain_q, gain_k, key_tiles, tile_counts, tile_valid):
    n_head = lax.axis_size("head")
    rows, width = queries.shape
    own_tiles = rows // TILE
    span_tiles = own_tiles * n_head
    heads = width // HD
    tiles, slots = key_tiles.shape
    listed = key_tiles.T

    smem = pl.BlockSpec(memory_space=pltpu.SMEM)
    vmem = pl.BlockSpec(memory_space=pltpu.VMEM)
    hbm = pl.BlockSpec(memory_space=pl.ANY)
    shape = (own_tiles, TILE, width)
    dma = pltpu.SemaphoreType.DMA

    def buffer(*lead, tail=(TILE, HD), kind=jnp.bfloat16):
        return pltpu.VMEM((*lead, *tail), kind)

    out = pl.pallas_call(
        functools.partial(kernel, n_head),
        out_shape=pltpu.VMEM(shape, jnp.bfloat16),
        in_specs=[smem] * 3 + [hbm] * 3 + [vmem] * 4,
        out_specs=hbm,
        scratch_shapes=[
            pltpu.VMEM(shape, jnp.bfloat16),
            pltpu.VMEM(shape, jnp.bfloat16),
            buffer(heads, own_tiles),
            buffer(heads, own_tiles),
            pltpu.VMEM((2 * SIDE, tiles), jnp.int32),
            pltpu.SMEM((2 * SIDE, tiles), jnp.int32),
            buffer(CORES, n_head, COLUMNS, own_tiles),
            buffer(CORES, n_head, COLUMNS, own_tiles),
            buffer(COLUMNS, own_tiles),
            buffer(COLUMNS, own_tiles),
            buffer(COLUMNS, own_tiles, tail=(TILE, slots * TILE)),
            buffer(COLUMNS, own_tiles, tail=(TILE, 1), kind=jnp.float32),
            buffer(SIDE, span_tiles),
            buffer(SIDE, span_tiles),
            buffer(SIDE * CORES, SIDE),
            buffer(SIDE * CORES, SIDE),
            buffer(span_tiles),
            buffer(2, len(HOPS), SIDE),
            buffer(span_tiles),
            dma((3,)),
            dma((2,)),
            dma((3,)),
            dma((3, SIDE)),
            dma((2,)),
            dma((2, 4, SIDE)),
            dma((2,)),
            dma((2,)),
            dma((3,)),
            dma((3, n_head - 1)),
            dma((2,)),
            dma((2, 4)),
            dma((2,)),
            dma((2,)),
            dma((2,)),
            dma((2,)),
            dma((2,)),
        ],
        compiler_params=pltpu.CompilerParams(
            collective_id=0, has_side_effects=True, vmem_limit_bytes=58 << 20
        ),
    )(
        listed, tile_counts, tile_valid,
        queries.reshape(shape), keys.reshape(shape), values.reshape(shape),
        gain_q, gain_k, listed, tile_counts,
    )
    return out.reshape(rows, width)


def solution(mesh):
    placed = P(("seq", "head"), None)
    return jax.shard_map(
        on_device,
        mesh=mesh,
        in_specs=(placed, placed, placed, P(), P(), P(), P(), P()),
        out_specs=placed,
        check_vma=False,
    )
```

```python
import functools
import math

import jax
import jax.numpy as jnp
from jax import lax
from jax.experimental import pallas as pl
from jax.experimental.pallas import tpu as pltpu
from jax.sharding import PartitionSpec as P

HD = 128
TILE = 128
EPS = 1e-06
MASKED = -1e30
MESH = pl.DeviceIdType.MESH
LOG2E = math.log2(math.e)
SIDE = 4
CORES = 2
STRIDE = (SIDE * CORES, CORES)
COLUMNS = SIDE * SIDE
HOPS = ((2, 0), (2, 1), (1, 0), (3, 0), (1, 1), (3, 1), (0, 1))
CHUNKS = (0, 1, 3, 2)
GROUPS = 8
K, V, Q = 0, 1, 2


def schedule():
    return (
        [("send", V), ("scale", K), ("spread_k", 0), ("send", K)]
        + [("own_ring", V), ("own_ring", K), ("direct", K, 0), ("spread_v", 0)]
        + [("direct", K, q) for q in CHUNKS[1:]]
        + [("scale", Q), ("spread_q", 0), ("send", Q)]
        + [("pass_on", K, 0), ("ring_rest", 0), ("pass_on", K, 1), ("pass_on", K, 3)]
        + [("direct", V, 0), ("pass_on", K, 2), ("direct", V, 1), ("finish", K, 0), ("finish", K, 1)]
        + [("direct", V, 3), ("relay", 0), ("finish", K, 3), ("direct", V, 2), ("finish", K, 2)]
        + [("pick", 0), ("pass_on", V, 0), ("complete", K), ("weigh", 0), ("pass_on", V, 1)]
        + [("weigh", 1), ("weigh", 2), ("weigh", 3), ("pass_on", V, 3), ("weigh", 4), ("weigh", 5)]
        + [("pass_on", V, 2), ("finish", V, 0), ("finish", V, 1), ("weigh", 6), ("weigh", 7)]
        + [("finish", V, 3), ("attend", 0), ("finish", V, 2), ("complete", V), ("mix", 0)]
    )


def row_scale(rows_ref, width):
    total = jnp.zeros((rows_ref.shape[0], TILE, HD), jnp.float32)
    for g in range(width // HD):
        part = rows_ref[:, :, g * HD : (g + 1) * HD].astype(jnp.float32)
        total = total + part * part
    return lax.rsqrt(jnp.sum(total, axis=-1, keepdims=True) / width + EPS)


def find_tables(s, place, span_tiles, own_tiles, last_valid, listed_rows, count_row, found, tables):
    slots, tiles = listed_rows.shape
    used = lax.broadcasted_iota(jnp.int32, (slots, tiles), 0) < count_row[...][None]
    listed = jnp.where(used, listed_rows[...], -1)
    span_bits = span_tiles.bit_length() - 1
    owner = listed >> span_bits
    tile = listed & (span_tiles - 1)
    for kind in (K, V):
        for a in range(SIDE):
            source = s + (a - place[kind]) * STRIDE[kind]
            best = jnp.max(jnp.where(owner == source, tile, 0), axis=0, keepdims=True)
            found[pl.ds(kind * SIDE + a, 1), :] = best
    every = listed_rows[...]
    spread = every & (tiles - 1)
    z, y, c = spread >> (span_bits + 3), (spread >> (span_bits + 1)) & 3, (spread >> span_bits) & 1
    own_bits = own_tiles.bit_length() - 1
    column = (c * (span_tiles // own_tiles) + ((spread & (span_tiles - 1)) >> own_bits)) * COLUMNS + z * SIDE + y
    tables[0] = column * own_tiles + (spread & (own_tiles - 1))
    tables[1] = (y * CORES + c) * SIDE + z
    tables[2] = (z * CORES + c) * SIDE + y
    tables[3] = jnp.where(used, jnp.where(every == tiles - 1, last_valid, TILE), 0)
    best = found[...]
    for step in (1, 2, 4):
        best = jnp.maximum(best, pltpu.roll(best, tiles - step, 1))
    found[...] = best


def kernel(
    n_head,
    valid, q_hbm, k_hbm, v_hbm, gain_q, gain_k, listed_rows, count_row,
    o_ref,
    q_in, k_in, q_norm, k_norm, found, wanted, tables, look,
    col_k, col_v, col_q, col_out, weights, inverse,
    ring_k, ring_v, bank_k, bank_v, blk_q, picked, blk_out,
    in_sem, own_sem, m_send, m_recv, x_send, x_recv, c_send, c_recv,
    a_send, a_recv, r_send, r_recv, b_send, b_recv, o_send, o_recv, o_own,
):
    s = lax.axis_index("seq")
    x = lax.axis_index("head")
    place = (s // STRIDE[0], s // STRIDE[1] % SIDE)
    core = s % CORES
    here = place[0] * SIDE + place[1]
    own_tiles = q_hbm.shape[0]
    span_tiles = own_tiles * n_head
    half = span_tiles // 2
    width = q_hbm.shape[2]
    slots, tiles = listed_rows.shape
    mine = pl.ds(x * own_tiles, own_tiles)

    def slab(slot, first, count, lane=core):
        return pl.ds(((lane * n_head + slot) * COLUMNS + first) * own_tiles, count * own_tiles)

    raw = (k_in, None, q_in)
    norm = (k_norm, None, q_norm)
    gain = (gain_k, None, gain_q)
    col = (col_k, col_v, col_q)
    ring = (ring_k, ring_v)
    bank = (bank_k, bank_v)
    scales = {}

    def device(dz, dy, cores):
        z = lax.rem(place[0] + dz, SIDE)
        y = lax.rem(place[1] + dy, SIDE)
        return (z * STRIDE[0] + y * STRIDE[1] + lax.rem(core + cores, CORES), x)

    def crossing(kind, along, cross, cores):
        return device(along, cross, cores) if kind == K else device(cross, along, cores)

    def beside(o):
        return (s, lax.rem(x + o, n_head))

    def columns(head):
        return pl.ds(pl.multiple_of(head * HD, HD), HD)

    def remote(src, dst, send_sem, recv_sem, dest):
        pltpu.make_async_remote_copy(
            src_ref=src, dst_ref=dst, send_sem=send_sem, recv_sem=recv_sem,
            device_id=dest, device_id_type=MESH,
        ).start()

    def await_bytes(ref, sem):
        pltpu.make_async_copy(ref, ref, sem).wait()

    load_k = pltpu.make_async_copy(k_hbm, k_in, in_sem.at[0])
    load_q = pltpu.make_async_copy(q_hbm, q_in, in_sem.at[1])
    load_k.start()
    load_q.start()
    rest_head = COLUMNS + x
    own_rest = pltpu.make_async_copy(
        v_hbm.at[:, :, columns(rest_head)], ring_v.at[place[1], mine], own_sem.at[0]
    )
    own_col = pltpu.make_async_copy(
        v_hbm.at[:, :, columns(here)], col_v.at[slab(x, here, 1)], own_sem.at[1]
    )
    own_rest.start()
    own_col.start()

    barrier = pltpu.get_barrier_semaphore()
    friends = [beside(o) for o in range(1, n_head)]
    friends += [device(dz, dy, 0) for dz in range(SIDE) for dy in range(SIDE) if dz + dy]
    friends += [device(0, dy, 1) for dy in range(SIDE)] + [device(dz, 0, 1) for dz in range(1, SIDE)]
    for friend in friends:
        pl.semaphore_signal(barrier, inc=1, device_id=friend, device_id_type=MESH)
    find_tables(
        s, place, span_tiles, own_tiles, valid[tiles - 1], listed_rows, count_row, found, tables
    )
    to_smem = pltpu.make_async_copy(found, wanted, in_sem.at[2])
    to_smem.start()
    tables_out = pltpu.make_async_copy(tables, look, in_sem.at[3])
    tables_out.start()
    pl.semaphore_wait(barrier, len(friends))

    def scale(kind):
        (load_k if kind == K else load_q).wait()
        scales[kind] = row_scale(raw[kind], width)
        if kind == Q:
            scales[kind] = scales[kind] * (HD**-0.5 * LOG2E)

    def normalised(kind, head):
        cols = columns(head)
        rows = raw[kind][:, :, cols].astype(jnp.float32)
        return (rows * scales[kind] * gain[kind][cols][None, None]).astype(jnp.bfloat16)

    def source(kind, head):
        if kind == V:
            return v_hbm.at[:, :, columns(head)]
        norm[kind][head] = normalised(kind, head)
        return norm[kind].at[head]

    def to_columns(kind):
        for dz in CHUNKS:
            for dy in CHUNKS:
                if dz + dy:
                    z, y = lax.rem(place[0] + dz, SIDE), lax.rem(place[1] + dy, SIDE)
                    landing = col_q.at[here] if kind == Q else col[kind].at[slab(x, here, 1)]
                    remote(
                        source(kind, z * SIDE + y), landing, m_send.at[kind],
                        m_recv.at[kind, (SIDE - dz) % SIDE], device(dz, dy, 0),
                    )

    def spread_k(_):
        col_k[slab(x, here, 1)] = normalised(K, here)
        to_columns(K)

    def spread_v(_):
        to_columns(V)

    def spread_q(_):
        col_q[here] = normalised(Q, here)
        to_columns(Q)

    def chunk(slot, q, first=0, count=SIDE):
        return slab(slot, lax.rem(place[0] + q, SIDE) * SIDE + first, count)

    def chunk_wait(kind, q):
        landed = col_k.at[pl.ds(0, (SIDE - 1 if q == 0 else SIDE) * own_tiles)]
        await_bytes(landed, m_recv.at[kind, q])

    def across(kind, slot, q):
        ref = col[kind].at[chunk(slot, q)]
        remote(ref, ref, c_send.at[kind], c_recv.at[kind], device(0, 0, 1))

    def direct(kind, q):
        if kind == V and q == 0:
            own_col.wait()
        chunk_wait(kind, q)
        ref = col[kind].at[chunk(x, q)]
        for n, along in enumerate((1, SIDE - 1)):
            remote(ref, ref, x_send.at[kind], x_recv.at[kind, n, q], beside(along))
        across(kind, x, q)

    def pass_on(kind, q):
        for n, along in enumerate((1, SIDE - 1)):
            slot = lax.rem(x + SIDE - along, SIDE)
            await_bytes(col[kind].at[chunk(slot, q)], x_recv.at[kind, n, q])
            ref = col[kind].at[chunk(slot, q, n * (SIDE // 2), SIDE // 2)]
            remote(ref, ref, x_send.at[kind], x_recv.at[kind, 2 + n, q], beside(along))
            across(kind, slot, q)

    def finish(kind, q):
        slot = lax.rem(x + SIDE // 2, SIDE)
        for n in (0, 1):
            ref = col[kind].at[chunk(slot, q, n * (SIDE // 2), SIDE // 2)]
            await_bytes(ref, x_recv.at[kind, 2 + n, q])
        across(kind, slot, q)

    def complete(kind):
        await_bytes(col[kind].at[slab(0, 0, n_head * COLUMNS, 1 - core)], c_recv.at[kind])
        if kind == K:
            for q in CHUNKS:
                chunk_wait(Q, q)

    lane = lax.broadcasted_iota(jnp.int32, (1, TILE), 1)

    def key_bias(row):
        return jnp.concatenate(
            [jnp.where(lane < look[3, e, row], 0.0, MASKED) for e in range(slots)], axis=1
        )

    def softmax(query, keys, bias):
        scores = lax.dot_general(
            query, jnp.concatenate(keys, axis=0), (((1,), (1,)), ((), ())),
            preferred_element_type=jnp.float32,
        ) + bias
        rows = jnp.exp2(scores - jnp.max(scores, axis=1, keepdims=True))
        return rows.astype(jnp.bfloat16), 1.0 / jnp.sum(rows, axis=1, keepdims=True)

    def col_row(block, part):
        return (block * CORES + core) * span_tiles + x * own_tiles + part

    def weigh(group):
        each = COLUMNS // GROUPS

        @pl.loop(group * each, (group + 1) * each)
        def _(block):
            for part in range(own_tiles):
                row = col_row(block, part)
                keys = [col_k[look[0, e, row]] for e in range(slots)]
                rows, inv = softmax(col_q[block, part], keys, key_bias(row))
                weights[block, part] = rows
                inverse[block, part] = inv

    def mix(_):
        @pl.loop(0, COLUMNS)
        def _(step):
            off = 5 * (step + 1) % COLUMNS
            dz, dy = off // SIDE, off % SIDE
            z, y = lax.rem(place[0] + dz, SIDE), lax.rem(place[1] + dy, SIDE)
            block = z * SIDE + y
            for part in range(own_tiles):
                row = col_row(block, part)
                vals = [col_v[look[0, e, row]] for e in range(slots)]
                mixed = jnp.dot(
                    weights[block, part], jnp.concatenate(vals, axis=0),
                    preferred_element_type=jnp.float32,
                )
                col_out[block, part] = (mixed * inverse[block, part]).astype(jnp.bfloat16)

            @pl.when(off > 0)
            def _():
                remote(
                    col_out.at[block], o_ref.at[:, :, columns(here)], o_send.at[0], o_recv.at[0],
                    (z * STRIDE[0] + y * STRIDE[1] + core, x),
                )

        pltpu.make_async_copy(col_out.at[here], o_ref.at[:, :, columns(here)], o_own.at[0]).start()

    def home(kind):
        return blk_q if kind == Q else ring[kind].at[place[kind]]

    def send(kind):
        for o in (2, 1, 3):
            remote(
                source(kind, COLUMNS + lax.rem(x + o, n_head)), home(kind).at[mine],
                a_send.at[kind], a_recv.at[kind, o - 1], beside(o),
            )
        if kind == Q:
            blk_q[mine] = normalised(Q, rest_head)

    def arrived(kind, o):
        await_bytes(home(kind).at[mine], a_recv.at[kind, o - 1])

    def ring_copy(kind, slot, tiles, n, sem):
        ref = ring[kind].at[slot, tiles]
        along = (1, SIDE - 1)[n]
        remote(ref, ref, r_send.at[kind], r_recv.at[kind, sem], crossing(kind, along, 0, 0))

    def ring_piece(kind, o):
        tiles = pl.ds(lax.rem(x + n_head - o, n_head) * own_tiles, own_tiles)
        for n in (0, 1):
            ring_copy(kind, place[kind], tiles, n, n)

    def own_ring(kind):
        if kind == V:
            own_rest.wait()
        else:
            ring_k[place[K], mine] = normalised(K, rest_head)
        ring_piece(kind, 0)

    def ring_rest(_):
        for o in (1, 3, 2):
            for kind in (V, K):
                arrived(kind, o)
                ring_piece(kind, o)

    def relay(_):
        for kind in (K, V):
            for n in (0, 1):
                await_bytes(ring[kind].at[0], r_recv.at[kind, n])
        for kind in (K, V):
            for n, along in enumerate((1, SIDE - 1)):
                slot = lax.rem(place[kind] + SIDE - along, SIDE)
                ring_copy(kind, slot, pl.ds(n * half, half), n, 2 + n)

    def pick(_):
        to_smem.wait()
        tables_out.wait()
        for kind in (K, V):
            for n in (0, 1):
                await_bytes(ring[kind].at[0, pl.ds(0, half)], r_recv.at[kind, 2 + n])
        for n, (cross, cores) in enumerate(HOPS):
            for kind in (K, V):
                dest = crossing(kind, 0, cross, cores)
                for a in range(SIDE):
                    picked[kind, n, a] = ring[kind][a, wanted[kind * SIDE + a, dest[0] * span_tiles]]
                remote(
                    picked.at[kind, n], bank[kind].at[pl.ds((place[1 - kind] * CORES + core) * SIDE, SIDE)],
                    b_send.at[kind], b_recv.at[kind], dest,
                )
        for kind in (K, V):
            for a in range(SIDE):
                bank[kind][(place[1 - kind] * CORES + core) * SIDE + a] = ring[kind][
                    a, wanted[kind * SIDE + a, s * span_tiles]
                ]

    def attend(_):
        for o in range(1, n_head):
            arrived(Q, o)
        for kind in (K, V):
            await_bytes(bank[kind].at[pl.ds(0, len(HOPS) * SIDE)], b_recv.at[kind])

        @pl.loop(0, span_tiles)
        def _(step):
            o = n_head - 1 - step // own_tiles
            part = step % own_tiles
            dest = lax.rem(x + o, n_head)
            i = dest * own_tiles + part
            row = s * span_tiles + i
            mate = i + 1 - 2 * (i % 2)
            keys = [ring_k[place[K], i], ring_k[place[K], mate]]
            vals = [ring_v[place[V], i], ring_v[place[V], mate]]
            for e in range(2, slots):
                keys.append(bank_k[look[1, e, row]])
                vals.append(bank_v[look[2, e, row]])
            rows, inv = softmax(blk_q[i], keys, key_bias(row))
            mixed = jnp.dot(rows, jnp.concatenate(vals, axis=0), preferred_element_type=jnp.float32)
            blk_out[i] = (mixed * inv).astype(jnp.bfloat16)

            @pl.when((part == own_tiles - 1) & (o > 0))
            def _():
                remote(
                    blk_out.at[pl.ds(dest * own_tiles, own_tiles)], o_ref.at[:, :, columns(rest_head)],
                    o_send.at[1], o_recv.at[1], (s, dest),
                )

        pltpu.make_async_copy(blk_out.at[mine], o_ref.at[:, :, columns(rest_head)], o_own.at[1]).start()

    stages = dict(
        send=send, scale=scale, spread_k=spread_k, spread_v=spread_v, spread_q=spread_q,
        own_ring=own_ring, direct=direct, pass_on=pass_on, finish=finish, complete=complete,
        ring_rest=ring_rest, relay=relay, pick=pick, weigh=weigh, attend=attend, mix=mix,
    )
    for name, *args in schedule():
        stages[name](*args)

    away = col_q.at[pl.ds(0, COLUMNS - 1)]
    aside = blk_q.at[pl.ds(0, span_tiles - own_tiles)]
    for kind in (K, V, Q):
        await_bytes(away, m_send.at[kind])
        await_bytes(aside, a_send.at[kind])
    for kind in (K, V):
        await_bytes(col_k.at[slab(0, 0, 3 * COLUMNS, 0)], x_send.at[kind])
        await_bytes(col_k.at[slab(0, 0, n_head * COLUMNS, 0)], c_send.at[kind])
        await_bytes(ring_k.at[pl.ds(0, 3)], r_send.at[kind])
        await_bytes(picked.at[kind], b_send.at[kind])
    for n, (moved, kept, head) in enumerate(
        ((away, col_out.at[here], here), (aside, blk_out.at[mine], rest_head))
    ):
        await_bytes(moved, o_send.at[n])
        await_bytes(moved, o_recv.at[n])
        pltpu.make_async_copy(kept, o_ref.at[:, :, columns(head)], o_own.at[n]).wait()


def on_device(queries, keys, values, gain_q, gain_k, key_tiles, tile_counts, tile_valid):
    n_head = lax.axis_size("head")
    rows, width = queries.shape
    own_tiles = rows // TILE
    span_tiles = own_tiles * n_head
    heads = width // HD
    tiles, slots = key_tiles.shape
    listed = key_tiles.T

    smem = pl.BlockSpec(memory_space=pltpu.SMEM)
    vmem = pl.BlockSpec(memory_space=pltpu.VMEM)
    hbm = pl.BlockSpec(memory_space=pl.ANY)
    shape = (own_tiles, TILE, width)
    dma = pltpu.SemaphoreType.DMA

    def buffer(*lead, tail=(TILE, HD), kind=jnp.bfloat16):
        return pltpu.VMEM((*lead, *tail), kind)

    out = pl.pallas_call(
        functools.partial(kernel, n_head),
        out_shape=pltpu.VMEM(shape, jnp.bfloat16),
        in_specs=[smem] + [hbm] * 3 + [vmem] * 4,
        out_specs=hbm,
        scratch_shapes=[
            pltpu.VMEM(shape, jnp.bfloat16),
            pltpu.VMEM(shape, jnp.bfloat16),
            buffer(heads, own_tiles),
            buffer(heads, own_tiles),
            pltpu.VMEM((2 * SIDE, tiles), jnp.int32),
            pltpu.SMEM((2 * SIDE, tiles), jnp.int32),
            pltpu.VMEM((4, slots, tiles), jnp.int32),
            pltpu.SMEM((4, slots, tiles), jnp.int32),
            buffer(tiles),
            buffer(tiles),
            buffer(COLUMNS, own_tiles),
            buffer(COLUMNS, own_tiles),
            buffer(COLUMNS, own_tiles, tail=(TILE, slots * TILE)),
            buffer(COLUMNS, own_tiles, tail=(TILE, 1), kind=jnp.float32),
            buffer(SIDE, span_tiles),
            buffer(SIDE, span_tiles),
            buffer(SIDE * CORES * SIDE),
            buffer(SIDE * CORES * SIDE),
            buffer(span_tiles),
            buffer(2, len(HOPS), SIDE),
            buffer(span_tiles),
            dma((4,)),
            dma((2,)),
            dma((3,)),
            dma((3, SIDE)),
            dma((2,)),
            dma((2, 4, SIDE)),
            dma((2,)),
            dma((2,)),
            dma((3,)),
            dma((3, n_head - 1)),
            dma((2,)),
            dma((2, 4)),
            dma((2,)),
            dma((2,)),
            dma((2,)),
            dma((2,)),
            dma((2,)),
        ],
        compiler_params=pltpu.CompilerParams(
            collective_id=0, has_side_effects=True, vmem_limit_bytes=58 << 20
        ),
    )(
        tile_valid,
        queries.reshape(shape), keys.reshape(shape), values.reshape(shape),
        gain_q, gain_k, listed, tile_counts,
    )
    return out.reshape(rows, width)


def solution(mesh):
    placed = P(("seq", "head"), None)
    return jax.shard_map(
        on_device,
        mesh=mesh,
        in_specs=(placed, placed, placed, P(), P(), P(), P(), P()),
        out_specs=placed,
        check_vma=False,
    )
```

```python
import functools
import math

import jax
import jax.numpy as jnp
from jax import lax
from jax.experimental import pallas as pl
from jax.experimental.pallas import tpu as pltpu
from jax.sharding import PartitionSpec as P

HD = 128
TILE = 128
EPS = 1e-06
MASKED = -1e30
MESH = pl.DeviceIdType.MESH
LOG2E = math.log2(math.e)
SIDE = 4
CORES = 2
STRIDE = (SIDE * CORES, CORES)
COLUMNS = SIDE * SIDE
HOPS = ((2, 0), (2, 1), (1, 0), (3, 0), (1, 1), (3, 1), (0, 1))
CHUNKS = (0, 1, 3, 2)
GROUPS = 8
K, V, Q = 0, 1, 2


def schedule():
    return (
        [("send", V), ("early", V), ("spread_v", 0), ("own_ring", V), ("scale", K), ("own", K), ("early", K)]
        + [("send", K), ("spread_k", 0), ("own_ring", K), ("direct", V, 0), ("look_up", 0)]
        + [("direct", K, q) for q in CHUNKS]
        + [("spread_v", 1), ("spread_v", 3), ("spread_v", 2)]
        + [("pass_on", K, 0), ("ring_rest", 0), ("pass_on", K, 1), ("pass_on", K, 3)]
        + [("scale", Q), ("own", Q), ("spread_q", 0), ("send", Q)]
        + [("direct", V, 1), ("pass_on", K, 2), ("direct", V, 3), ("finish", K, 0), ("finish", K, 1)]
        + [("relay", 0), ("finish", K, 3), ("direct", V, 2), ("finish", K, 2)]
        + [("pick", 0), ("pass_on", V, 0), ("complete", K), ("weigh", 0), ("pass_on", V, 1)]
        + [("weigh", 1), ("weigh", 2), ("pass_on", V, 3), ("weigh", 3), ("weigh", 4), ("pass_on", V, 2)]
        + [("attend", 0), ("answer", 0), ("finish", V, 0), ("finish", V, 1), ("weigh", 5), ("weigh", 6), ("weigh", 7)]
        + [("finish", V, 3), ("finish", V, 2), ("complete", V), ("mix", 0)]
    )


def row_scale(rows_ref, width):
    total = jnp.zeros((rows_ref.shape[0], TILE, HD), jnp.float32)
    for g in range(width // HD):
        part = rows_ref[:, :, g * HD : (g + 1) * HD].astype(jnp.float32)
        total = total + part * part
    return lax.rsqrt(jnp.sum(total, axis=-1, keepdims=True) / width + EPS)


def find_tables(s, place, span_tiles, own_tiles, last_valid, listed_rows, count_row, found, tables):
    slots, tiles = listed_rows.shape
    used = lax.broadcasted_iota(jnp.int32, (slots, tiles), 0) < count_row[...][None]
    listed = jnp.where(used, listed_rows[...], -1)
    span_bits = span_tiles.bit_length() - 1
    owner = listed >> span_bits
    tile = listed & (span_tiles - 1)
    for kind in (K, V):
        for a in range(SIDE):
            source = s + (a - place[kind]) * STRIDE[kind]
            best = jnp.max(jnp.where(owner == source, tile, 0), axis=0, keepdims=True)
            found[pl.ds(kind * SIDE + a, 1), :] = best
    every = listed_rows[...]
    spread = every & (tiles - 1)
    z, y, c = spread >> (span_bits + 3), (spread >> (span_bits + 1)) & 3, (spread >> span_bits) & 1
    own_bits = own_tiles.bit_length() - 1
    column = (c * (span_tiles // own_tiles) + ((spread & (span_tiles - 1)) >> own_bits)) * COLUMNS + z * SIDE + y
    tables[0] = column * own_tiles + (spread & (own_tiles - 1))
    tables[1] = (y * CORES + c) * SIDE + z
    tables[2] = (z * CORES + c) * SIDE + y
    tables[3] = jnp.where(used, jnp.where(every == tiles - 1, last_valid, TILE), 0)
    best = found[...]
    for step in (1, 2, 4):
        best = jnp.maximum(best, pltpu.roll(best, tiles - step, 1))
    found[...] = best


def kernel(
    n_head,
    valid_hbm, q_hbm, k_hbm, v_hbm, gain_q_hbm, gain_k_hbm, listed_hbm, count_hbm,
    o_ref,
    valid, gain_q, gain_k, listed_rows, count_row, small_sem,
    q_in, k_in, q_norm, k_norm, found, wanted, tables, look,
    col_k, col_v, col_q, col_out, weights, inverse,
    ring_k, ring_v, bank_k, bank_v, blk_q, picked, blk_out,
    in_sem, own_sem, m_send, m_recv, x_send, x_recv, c_send, c_recv,
    a_send, a_recv, r_send, r_recv, b_send, b_recv, o_send, o_recv, o_own,
):
    s = lax.axis_index("seq")
    x = lax.axis_index("head")
    place = (s // STRIDE[0], s // STRIDE[1] % SIDE)
    core = s % CORES
    here = place[0] * SIDE + place[1]
    own_tiles = q_hbm.shape[0]
    span_tiles = own_tiles * n_head
    half = span_tiles // 2
    width = q_hbm.shape[2]
    slots, tiles = listed_rows.shape
    mine = pl.ds(x * own_tiles, own_tiles)

    def slab(slot, first, count, lane=core):
        return pl.ds(((lane * n_head + slot) * COLUMNS + first) * own_tiles, count * own_tiles)

    raw = (k_in, None, q_in)
    norm = (k_norm, None, q_norm)
    gain = (gain_k, None, gain_q)
    col = (col_k, col_v, col_q)
    ring = (ring_k, ring_v)
    bank = (bank_k, bank_v)
    scales = {}

    def device(dz, dy, cores):
        z = lax.rem(place[0] + dz, SIDE)
        y = lax.rem(place[1] + dy, SIDE)
        return (z * STRIDE[0] + y * STRIDE[1] + lax.rem(core + cores, CORES), x)

    def crossing(kind, along, cross, cores):
        return device(along, cross, cores) if kind == K else device(cross, along, cores)

    def beside(o):
        return (s, lax.rem(x + o, n_head))

    def columns(head):
        return pl.ds(pl.multiple_of(head * HD, HD), HD)

    def remote(src, dst, send_sem, recv_sem, dest):
        pltpu.make_async_remote_copy(
            src_ref=src, dst_ref=dst, send_sem=send_sem, recv_sem=recv_sem,
            device_id=dest, device_id_type=MESH,
        ).start()

    def await_bytes(ref, sem):
        pltpu.make_async_copy(ref, ref, sem).wait()

    load_k = pltpu.make_async_copy(k_hbm, k_in, in_sem.at[0])
    load_k.start()
    barrier = pltpu.get_barrier_semaphore()
    friends = [beside(o) for o in range(1, n_head)]
    friends += [device(dz, dy, 0) for dz in range(SIDE) for dy in range(SIDE) if dz + dy]
    friends += [device(0, dy, 1) for dy in range(SIDE)] + [device(dz, 0, 1) for dz in range(1, SIDE)]
    for friend in friends:
        pl.semaphore_signal(barrier, inc=1, device_id=friend, device_id_type=MESH)
    small = [
        pltpu.make_async_copy(src, dst, small_sem.at[n])
        for n, (src, dst) in enumerate((
            (gain_k_hbm, gain_k), (listed_hbm, listed_rows), (count_hbm, count_row),
            (valid_hbm, valid), (gain_q_hbm, gain_q),
        ))
    ]
    for copy in small:
        copy.start()
    load_q = pltpu.make_async_copy(q_hbm, q_in, in_sem.at[1])
    load_q.start()
    rest_head = COLUMNS + x
    own_rest = pltpu.make_async_copy(
        v_hbm.at[:, :, columns(rest_head)], ring_v.at[place[1], mine], own_sem.at[0]
    )
    own_col = pltpu.make_async_copy(
        v_hbm.at[:, :, columns(here)], col_v.at[slab(x, here, 1)], own_sem.at[1]
    )
    own_rest.start()
    own_col.start()

    pl.semaphore_wait(barrier, len(friends))

    to_smem = pltpu.make_async_copy(found, wanted, in_sem.at[2])
    tables_out = pltpu.make_async_copy(tables, look, in_sem.at[3])

    def look_up(_):
        for copy in small[1:4]:
            copy.wait()
        find_tables(
            s, place, span_tiles, own_tiles, valid[tiles - 1], listed_rows, count_row, found, tables
        )
        to_smem.start()
        tables_out.start()

    def scale(kind):
        (load_k if kind == K else load_q).wait()
        small[0 if kind == K else 4].wait()
        scales[kind] = row_scale(raw[kind], width)
        if kind == Q:
            scales[kind] = scales[kind] * (HD**-0.5 * LOG2E)

    def normalised(kind, head):
        cols = columns(head)
        rows = raw[kind][:, :, cols].astype(jnp.float32)
        return (rows * scales[kind] * gain[kind][cols][None, None]).astype(jnp.bfloat16)

    def source(kind, head):
        if kind == V:
            return v_hbm.at[:, :, columns(head)]
        norm[kind][head] = normalised(kind, head)
        return norm[kind].at[head]

    def to_columns(kind, q):
        dz = (SIDE - q) % SIDE
        for dy in CHUNKS:
            if dz + dy:
                z, y = lax.rem(place[0] + dz, SIDE), lax.rem(place[1] + dy, SIDE)
                landing = col_q.at[here] if kind == Q else col[kind].at[slab(x, here, 1)]
                remote(
                    source(kind, z * SIDE + y), landing, m_send.at[kind],
                    m_recv.at[kind, q], device(dz, dy, 0),
                )

    def own(kind):
        if kind == K:
            col_k[slab(x, here, 1)] = normalised(K, here)
        else:
            col_q[here] = normalised(Q, here)

    def spread_k(_):
        for q in CHUNKS:
            to_columns(K, q)

    def spread_v(q):
        to_columns(V, q)

    def spread_q(_):
        for q in CHUNKS:
            to_columns(Q, q)

    def chunk(slot, q, first=0, count=SIDE):
        return slab(slot, lax.rem(place[0] + q, SIDE) * SIDE + first, count)

    def chunk_wait(kind, q):
        landed = col_k.at[pl.ds(0, (SIDE - 1 if q == 0 else SIDE) * own_tiles)]
        await_bytes(landed, m_recv.at[kind, q])

    def across(kind, slot, q):
        ref = col[kind].at[chunk(slot, q)]
        remote(ref, ref, c_send.at[kind], c_recv.at[kind], device(0, 0, 1))

    def around(kind, q, rows):
        ref = col[kind].at[rows]
        for n, along in enumerate((1, SIDE - 1)):
            remote(ref, ref, x_send.at[kind], x_recv.at[kind, n, q], beside(along))

    def early(kind):
        if kind == V:
            own_col.wait()
        around(kind, 0, slab(x, here, 1))

    def direct(kind, q):
        chunk_wait(kind, q)
        if q == 0:
            for dy in (1, 3, 2):
                around(kind, q, slab(x, place[0] * SIDE + lax.rem(place[1] + dy, SIDE), 1))
        else:
            around(kind, q, chunk(x, q))
        across(kind, x, q)

    def pass_on(kind, q):
        for n, along in enumerate((1, SIDE - 1)):
            slot = lax.rem(x + SIDE - along, SIDE)
            await_bytes(col[kind].at[chunk(slot, q)], x_recv.at[kind, n, q])
            ref = col[kind].at[chunk(slot, q, n * (SIDE // 2), SIDE // 2)]
            remote(ref, ref, x_send.at[kind], x_recv.at[kind, 2 + n, q], beside(along))
            across(kind, slot, q)

    def finish(kind, q):
        slot = lax.rem(x + SIDE // 2, SIDE)
        for n in (0, 1):
            ref = col[kind].at[chunk(slot, q, n * (SIDE // 2), SIDE // 2)]
            await_bytes(ref, x_recv.at[kind, 2 + n, q])
        across(kind, slot, q)

    def complete(kind):
        await_bytes(col[kind].at[slab(0, 0, n_head * COLUMNS, 1 - core)], c_recv.at[kind])
        if kind == K:
            for q in CHUNKS:
                chunk_wait(Q, q)

    lane = lax.broadcasted_iota(jnp.int32, (1, TILE), 1)

    def key_bias(row):
        return jnp.concatenate(
            [jnp.where(lane < look[3, e, row], 0.0, MASKED) for e in range(slots)], axis=1
        )

    def softmax(query, keys, bias):
        scores = lax.dot_general(
            query, jnp.concatenate(keys, axis=0), (((1,), (1,)), ((), ())),
            preferred_element_type=jnp.float32,
        ) + bias
        rows = jnp.exp2(scores - jnp.max(scores, axis=1, keepdims=True))
        return rows.astype(jnp.bfloat16), 1.0 / jnp.sum(rows, axis=1, keepdims=True)

    def col_row(block, part):
        return (block * CORES + core) * span_tiles + x * own_tiles + part

    def weigh(group):
        each = COLUMNS // GROUPS

        @pl.loop(group * each, (group + 1) * each)
        def _(block):
            for part in range(own_tiles):
                row = col_row(block, part)
                keys = [col_k[look[0, e, row]] for e in range(slots)]
                rows, inv = softmax(col_q[block, part], keys, key_bias(row))
                weights[block, part] = rows
                inverse[block, part] = inv

    def mix(_):
        @pl.loop(0, COLUMNS)
        def _(step):
            off = 5 * (step + 1) % COLUMNS
            dz, dy = off // SIDE, off % SIDE
            z, y = lax.rem(place[0] + dz, SIDE), lax.rem(place[1] + dy, SIDE)
            block = z * SIDE + y
            for part in range(own_tiles):
                row = col_row(block, part)
                vals = [col_v[look[0, e, row]] for e in range(slots)]
                mixed = jnp.dot(
                    weights[block, part], jnp.concatenate(vals, axis=0),
                    preferred_element_type=jnp.float32,
                )
                col_out[block, part] = (mixed * inverse[block, part]).astype(jnp.bfloat16)

            @pl.when(off > 0)
            def _():
                remote(
                    col_out.at[block], o_ref.at[:, :, columns(here)], o_send.at[0], o_recv.at[0],
                    (z * STRIDE[0] + y * STRIDE[1] + core, x),
                )

        pltpu.make_async_copy(col_out.at[here], o_ref.at[:, :, columns(here)], o_own.at[0]).start()

    def home(kind):
        return blk_q if kind == Q else ring[kind].at[place[kind]]

    def send(kind):
        for o in (2, 1, 3):
            remote(
                source(kind, COLUMNS + lax.rem(x + o, n_head)), home(kind).at[mine],
                a_send.at[kind], a_recv.at[kind, o - 1], beside(o),
            )
        if kind == Q:
            blk_q[mine] = normalised(Q, rest_head)

    def arrived(kind, o):
        await_bytes(home(kind).at[mine], a_recv.at[kind, o - 1])

    def ring_copy(kind, slot, tiles, n, sem):
        ref = ring[kind].at[slot, tiles]
        along = (1, SIDE - 1)[n]
        remote(ref, ref, r_send.at[kind], r_recv.at[kind, sem], crossing(kind, along, 0, 0))

    def ring_piece(kind, o):
        tiles = pl.ds(lax.rem(x + n_head - o, n_head) * own_tiles, own_tiles)
        for n in (0, 1):
            ring_copy(kind, place[kind], tiles, n, n)

    def own_ring(kind):
        if kind == V:
            own_rest.wait()
        else:
            ring_k[place[K], mine] = normalised(K, rest_head)
        ring_piece(kind, 0)

    def ring_rest(_):
        for o in (1, 3, 2):
            for kind in (V, K):
                arrived(kind, o)
                ring_piece(kind, o)

    def relay(_):
        for kind in (K, V):
            for n in (0, 1):
                await_bytes(ring[kind].at[0], r_recv.at[kind, n])
        for kind in (K, V):
            for n, along in enumerate((1, SIDE - 1)):
                slot = lax.rem(place[kind] + SIDE - along, SIDE)
                ring_copy(kind, slot, pl.ds(n * half, half), n, 2 + n)

    def pick(_):
        to_smem.wait()
        tables_out.wait()
        for kind in (K, V):
            for n in (0, 1):
                await_bytes(ring[kind].at[0, pl.ds(0, half)], r_recv.at[kind, 2 + n])
        for n, (cross, cores) in enumerate(HOPS):
            for kind in (K, V):
                dest = crossing(kind, 0, cross, cores)
                for a in range(SIDE):
                    picked[kind, n, a] = ring[kind][a, wanted[kind * SIDE + a, dest[0] * span_tiles]]
                remote(
                    picked.at[kind, n], bank[kind].at[pl.ds((place[1 - kind] * CORES + core) * SIDE, SIDE)],
                    b_send.at[kind], b_recv.at[kind], dest,
                )
        for kind in (K, V):
            for a in range(SIDE):
                bank[kind][(place[1 - kind] * CORES + core) * SIDE + a] = ring[kind][
                    a, wanted[kind * SIDE + a, s * span_tiles]
                ]

    def attend(_):
        for o in range(1, n_head):
            arrived(Q, o)
        for kind in (K, V):
            await_bytes(bank[kind].at[pl.ds(0, len(HOPS) * SIDE)], b_recv.at[kind])

        @pl.loop(0, span_tiles)
        def _(step):
            i = step
            row = s * span_tiles + i
            mate = i + 1 - 2 * (i % 2)
            keys = [ring_k[place[K], i], ring_k[place[K], mate]]
            vals = [ring_v[place[V], i], ring_v[place[V], mate]]
            for e in range(2, slots):
                keys.append(bank_k[look[1, e, row]])
                vals.append(bank_v[look[2, e, row]])
            rows, inv = softmax(blk_q[i], keys, key_bias(row))
            mixed = jnp.dot(rows, jnp.concatenate(vals, axis=0), preferred_element_type=jnp.float32)
            blk_out[i] = (mixed * inv).astype(jnp.bfloat16)

    def answer(_):
        for o in (2, 1, 3):
            dest = lax.rem(x + o, n_head)
            remote(
                blk_out.at[pl.ds(dest * own_tiles, own_tiles)], o_ref.at[:, :, columns(rest_head)],
                o_send.at[1], o_recv.at[1], beside(o),
            )
        pltpu.make_async_copy(blk_out.at[mine], o_ref.at[:, :, columns(rest_head)], o_own.at[1]).start()

    stages = dict(
        send=send, scale=scale, look_up=look_up, answer=answer, own=own, early=early, spread_k=spread_k, spread_v=spread_v, spread_q=spread_q,
        own_ring=own_ring, direct=direct, pass_on=pass_on, finish=finish, complete=complete,
        ring_rest=ring_rest, relay=relay, pick=pick, weigh=weigh, attend=attend, mix=mix,
    )
    for name, *args in schedule():
        stages[name](*args)

    away = col_q.at[pl.ds(0, COLUMNS - 1)]
    aside = blk_q.at[pl.ds(0, span_tiles - own_tiles)]
    for kind in (K, V, Q):
        await_bytes(away, m_send.at[kind])
        await_bytes(aside, a_send.at[kind])
    for kind in (K, V):
        await_bytes(col_k.at[slab(0, 0, 3 * COLUMNS, 0)], x_send.at[kind])
        await_bytes(col_k.at[slab(0, 0, n_head * COLUMNS, 0)], c_send.at[kind])
        await_bytes(ring_k.at[pl.ds(0, 3)], r_send.at[kind])
        await_bytes(picked.at[kind], b_send.at[kind])
    for n, (moved, kept, head) in enumerate(
        ((away, col_out.at[here], here), (aside, blk_out.at[mine], rest_head))
    ):
        await_bytes(moved, o_send.at[n])
        await_bytes(moved, o_recv.at[n])
        pltpu.make_async_copy(kept, o_ref.at[:, :, columns(head)], o_own.at[n]).wait()


def on_device(queries, keys, values, gain_q, gain_k, key_tiles, tile_counts, tile_valid):
    n_head = lax.axis_size("head")
    rows, width = queries.shape
    own_tiles = rows // TILE
    span_tiles = own_tiles * n_head
    heads = width // HD
    tiles, slots = key_tiles.shape
    listed = key_tiles.T

    hbm = pl.BlockSpec(memory_space=pl.ANY)
    shape = (own_tiles, TILE, width)
    dma = pltpu.SemaphoreType.DMA

    def buffer(*lead, tail=(TILE, HD), kind=jnp.bfloat16):
        return pltpu.VMEM((*lead, *tail), kind)

    out = pl.pallas_call(
        functools.partial(kernel, n_head),
        out_shape=pltpu.VMEM(shape, jnp.bfloat16),
        in_specs=[hbm] * 8,
        out_specs=hbm,
        scratch_shapes=[
            pltpu.SMEM((tiles,), jnp.int32),
            pltpu.VMEM((width,), jnp.float32),
            pltpu.VMEM((width,), jnp.float32),
            pltpu.VMEM((slots, tiles), jnp.int32),
            pltpu.VMEM((tiles,), jnp.int32),
            pltpu.SemaphoreType.DMA((5,)),
            pltpu.VMEM(shape, jnp.bfloat16),
            pltpu.VMEM(shape, jnp.bfloat16),
            buffer(heads, own_tiles),
            buffer(heads, own_tiles),
            pltpu.VMEM((2 * SIDE, tiles), jnp.int32),
            pltpu.SMEM((2 * SIDE, tiles), jnp.int32),
            pltpu.VMEM((4, slots, tiles), jnp.int32),
            pltpu.SMEM((4, slots, tiles), jnp.int32),
            buffer(tiles),
            buffer(tiles),
            buffer(COLUMNS, own_tiles),
            buffer(COLUMNS, own_tiles),
            buffer(COLUMNS, own_tiles, tail=(TILE, slots * TILE)),
            buffer(COLUMNS, own_tiles, tail=(TILE, 1), kind=jnp.float32),
            buffer(SIDE, span_tiles),
            buffer(SIDE, span_tiles),
            buffer(SIDE * CORES * SIDE),
            buffer(SIDE * CORES * SIDE),
            buffer(span_tiles),
            buffer(2, len(HOPS), SIDE),
            buffer(span_tiles),
            dma((4,)),
            dma((2,)),
            dma((3,)),
            dma((3, SIDE)),
            dma((2,)),
            dma((2, 4, SIDE)),
            dma((2,)),
            dma((2,)),
            dma((3,)),
            dma((3, n_head - 1)),
            dma((2,)),
            dma((2, 4)),
            dma((2,)),
            dma((2,)),
            dma((2,)),
            dma((2,)),
            dma((2,)),
        ],
        compiler_params=pltpu.CompilerParams(
            collective_id=0, has_side_effects=True, vmem_limit_bytes=58 << 20
        ),
    )(
        tile_valid,
        queries.reshape(shape), keys.reshape(shape), values.reshape(shape),
        gain_q, gain_k, listed, tile_counts,
    )
    return out.reshape(rows, width)


def solution(mesh):
    placed = P(("seq", "head"), None)
    return jax.shard_map(
        on_device,
        mesh=mesh,
        in_specs=(placed, placed, placed, P(), P(), P(), P(), P()),
        out_specs=placed,
        check_vma=False,
    )
```

```python
import functools
import math

import jax
import jax.numpy as jnp
from jax import lax
from jax.experimental import pallas as pl
from jax.experimental.pallas import tpu as pltpu
from jax.sharding import PartitionSpec as P

HD = 128
TILE = 128
EPS = 1e-06
MASKED = -1e30
MESH = pl.DeviceIdType.MESH
LOG2E = math.log2(math.e)
SIDE = 4
CORES = 2
STRIDE = (SIDE * CORES, CORES)
COLUMNS = SIDE * SIDE
HOPS = ((2, 0), (2, 1), (1, 0), (3, 0), (1, 1), (3, 1), (0, 1))
CHUNKS = (0, 1, 3, 2)
GROUPS = 8
K, V, Q, W = 0, 1, 2, 3
HALF = HD // 2


def schedule():
    return (
        [("send", V), ("scale", K), ("own", K), ("early", K), ("send", K), ("spread_k", 0)]
        + [("own_ring", V), ("own_ring", K), ("look_up", 0)]
        + [("direct", K, q) for q in CHUNKS]
        + [("halve", 0)] + [("spread_v", V, q) for q in CHUNKS]
        + [("pass_on", K, 0), ("ring_rest", 0), ("pass_on", K, 1), ("pass_on", K, 3)]
        + [("scale", Q), ("own", Q), ("spread_q", 0), ("send", Q)]
        + [("direct", V, 0), ("pass_on", K, 2), ("direct", V, 1), ("finish", K, 0), ("finish", K, 1)]
        + [("spread_v", W, q) for q in CHUNKS]
        + [("direct", V, 3), ("relay", 0), ("finish", K, 3), ("direct", V, 2), ("finish", K, 2)]
        + [("pick", 0), ("pass_on", V, 0), ("direct", W, 0), ("complete", K), ("weigh", 0)]
        + [("pass_on", V, 1), ("direct", W, 1), ("weigh", 1), ("pass_on", V, 3), ("direct", W, 3), ("weigh", 2)]
        + [("pass_on", V, 2), ("direct", W, 2), ("weigh", 3), ("finish", V, 0), ("finish", V, 1), ("weigh", 4)]
        + [("attend", 0), ("pass_on", W, 0), ("finish", V, 3), ("weigh", 5), ("finish", V, 2), ("weigh", 6), ("weigh", 7)]
        + [("pass_on", W, 1), ("pass_on", W, 3), ("pass_on", W, 2), ("answer", 0)]
        + [("complete", V), ("mix", V, 0), ("finish", W, 0), ("mix", V, 1)]
        + [("finish", W, 1), ("finish", W, 3), ("finish", W, 2)]
        + [("complete", W), ("mix", W, 0), ("mix", W, 1), ("join", 0)]
    )


def row_scale(rows_ref, width):
    total = jnp.zeros((rows_ref.shape[0], TILE, HD), jnp.float32)
    for g in range(width // HD):
        part = rows_ref[:, :, g * HD : (g + 1) * HD].astype(jnp.float32)
        total = total + part * part
    return lax.rsqrt(jnp.sum(total, axis=-1, keepdims=True) / width + EPS)


def find_tables(s, place, span_tiles, own_tiles, last_valid, listed_rows, count_row, found, tables):
    slots, tiles = listed_rows.shape
    used = lax.broadcasted_iota(jnp.int32, (slots, tiles), 0) < count_row[...][None]
    listed = jnp.where(used, listed_rows[...], -1)
    span_bits = span_tiles.bit_length() - 1
    owner = listed >> span_bits
    tile = listed & (span_tiles - 1)
    for kind in (K, V):
        for a in range(SIDE):
            source = s + (a - place[kind]) * STRIDE[kind]
            best = jnp.max(jnp.where(owner == source, tile, 0), axis=0, keepdims=True)
            found[pl.ds(kind * SIDE + a, 1), :] = best
    every = listed_rows[...]
    spread = every & (tiles - 1)
    z, y, c = spread >> (span_bits + 3), (spread >> (span_bits + 1)) & 3, (spread >> span_bits) & 1
    own_bits = own_tiles.bit_length() - 1
    column = (c * (span_tiles // own_tiles) + ((spread & (span_tiles - 1)) >> own_bits)) * COLUMNS + z * SIDE + y
    tables[0] = column * own_tiles + (spread & (own_tiles - 1))
    tables[1] = (y * CORES + c) * SIDE + z
    tables[2] = (z * CORES + c) * SIDE + y
    tables[3] = jnp.where(used, jnp.where(every == tiles - 1, last_valid, TILE), 0)
    best = found[...]
    for step in (1, 2, 4):
        best = jnp.maximum(best, pltpu.roll(best, tiles - step, 1))
    found[...] = best


def kernel(
    n_head,
    valid_hbm, q_hbm, k_hbm, v_hbm, gain_q_hbm, gain_k_hbm, listed_hbm, count_hbm,
    o_ref,
    valid, gain_q, gain_k, listed_rows, count_row, small_sem,
    q_in, k_in, v_in, q_norm, k_norm, v_half, found, wanted, tables, look,
    col_k, col_v, col_w, col_q, col_out, landed, weights, inverse,
    ring_k, ring_v, bank_k, bank_v, blk_q, picked, blk_out,
    in_sem, own_sem, m_send, m_recv, x_send, x_recv, c_send, c_recv,
    a_send, a_recv, r_send, r_recv, b_send, b_recv, o_send, o_recv, o_own,
):
    s = lax.axis_index("seq")
    x = lax.axis_index("head")
    place = (s // STRIDE[0], s // STRIDE[1] % SIDE)
    core = s % CORES
    here = place[0] * SIDE + place[1]
    own_tiles = q_hbm.shape[0]
    span_tiles = own_tiles * n_head
    half = span_tiles // 2
    width = q_hbm.shape[2]
    slots, tiles = listed_rows.shape
    mine = pl.ds(x * own_tiles, own_tiles)

    def slab(slot, first, count, lane=core):
        return pl.ds(((lane * n_head + slot) * COLUMNS + first) * own_tiles, count * own_tiles)

    raw = (k_in, None, q_in)
    norm = (k_norm, None, q_norm)
    gain = (gain_k, None, gain_q)
    col = (col_k, col_v, col_q, col_w)
    ring = (ring_k, ring_v)
    bank = (bank_k, bank_v)
    scales = {}

    def device(dz, dy, cores):
        z = lax.rem(place[0] + dz, SIDE)
        y = lax.rem(place[1] + dy, SIDE)
        return (z * STRIDE[0] + y * STRIDE[1] + lax.rem(core + cores, CORES), x)

    def crossing(kind, along, cross, cores):
        return device(along, cross, cores) if kind == K else device(cross, along, cores)

    def beside(o):
        return (s, lax.rem(x + o, n_head))

    def columns(head):
        return pl.ds(pl.multiple_of(head * HD, HD), HD)

    def remote(src, dst, send_sem, recv_sem, dest):
        pltpu.make_async_remote_copy(
            src_ref=src, dst_ref=dst, send_sem=send_sem, recv_sem=recv_sem,
            device_id=dest, device_id_type=MESH,
        ).start()

    def await_bytes(ref, sem):
        pltpu.make_async_copy(ref, ref, sem).wait()

    load_k = pltpu.make_async_copy(k_hbm, k_in, in_sem.at[0])
    load_k.start()
    barrier = pltpu.get_barrier_semaphore()
    friends = [beside(o) for o in range(1, n_head)]
    friends += [device(dz, dy, 0) for dz in range(SIDE) for dy in range(SIDE) if dz + dy]
    friends += [device(0, dy, 1) for dy in range(SIDE)] + [device(dz, 0, 1) for dz in range(1, SIDE)]
    for friend in friends:
        pl.semaphore_signal(barrier, inc=1, device_id=friend, device_id_type=MESH)
    small = [
        pltpu.make_async_copy(src, dst, small_sem.at[n])
        for n, (src, dst) in enumerate((
            (gain_k_hbm, gain_k), (listed_hbm, listed_rows), (count_hbm, count_row),
            (valid_hbm, valid), (gain_q_hbm, gain_q),
        ))
    ]
    for copy in small:
        copy.start()
    load_q = pltpu.make_async_copy(q_hbm, q_in, in_sem.at[1])
    load_q.start()
    rest_head = COLUMNS + x
    own_rest = pltpu.make_async_copy(
        v_hbm.at[:, :, columns(rest_head)], ring_v.at[place[1], mine], own_sem.at[0]
    )
    load_v = pltpu.make_async_copy(v_hbm, v_in, own_sem.at[1])
    own_rest.start()
    load_v.start()

    pl.semaphore_wait(barrier, len(friends))

    to_smem = pltpu.make_async_copy(found, wanted, in_sem.at[2])
    tables_out = pltpu.make_async_copy(tables, look, in_sem.at[3])

    def look_up(_):
        for copy in small[1:4]:
            copy.wait()
        find_tables(
            s, place, span_tiles, own_tiles, valid[tiles - 1], listed_rows, count_row, found, tables
        )
        to_smem.start()
        tables_out.start()

    def scale(kind):
        (load_k if kind == K else load_q).wait()
        small[0 if kind == K else 4].wait()
        scales[kind] = row_scale(raw[kind], width)
        if kind == Q:
            scales[kind] = scales[kind] * (HD**-0.5 * LOG2E)

    def normalised(kind, head):
        cols = columns(head)
        rows = raw[kind][:, :, cols].astype(jnp.float32)
        return (rows * scales[kind] * gain[kind][cols][None, None]).astype(jnp.bfloat16)

    def source(kind, head):
        if kind == V:
            return v_hbm.at[:, :, columns(head)]
        norm[kind][head] = normalised(kind, head)
        return norm[kind].at[head]

    def to_columns(kind, q):
        dz = (SIDE - q) % SIDE
        for dy in CHUNKS:
            if dz + dy:
                z, y = lax.rem(place[0] + dz, SIDE), lax.rem(place[1] + dy, SIDE)
                landing = col_q.at[here] if kind == Q else col[kind].at[slab(x, here, 1)]
                head = z * SIDE + y
                part = v_half.at[kind // W, head] if kind in (V, W) else source(kind, head)
                remote(
                    part, landing, m_send.at[kind],
                    m_recv.at[kind, q], device(dz, dy, 0),
                )

    def own(kind):
        if kind == K:
            col_k[slab(x, here, 1)] = normalised(K, here)
        else:
            col_q[here] = normalised(Q, here)

    def spread_k(_):
        for q in CHUNKS:
            to_columns(K, q)

    def halve(_):
        load_v.wait()
        shape = (2 * HD, 2 * HD)
        i, j = lax.broadcasted_iota(jnp.int32, shape, 0), lax.broadcasted_iota(jnp.int32, shape, 1)
        target = i % HALF + HALF * (i // HD) + HD * (i // HALF % 2)
        mover = jnp.where(j == target, 1.0, 0.0).astype(jnp.bfloat16)
        for head in range(COLUMNS):
            rows = v_in[:, :, head * HD : (head + 1) * HD]
            rows = jnp.concatenate([rows[:, :HALF], rows[:, HALF:]], axis=2).reshape(own_tiles * HALF, 2 * HD)
            moved = jnp.dot(rows, mover, preferred_element_type=jnp.float32).astype(jnp.bfloat16)
            for n in (0, 1):
                v_half[n, head] = moved[:, n * HD : (n + 1) * HD].reshape(own_tiles, HALF, HD)
        for n, ref in enumerate((col_v, col_w)):
            ref[slab(x, here, 1)] = v_half[n, here]

    def spread_v(kind, q):
        to_columns(kind, q)

    def spread_q(_):
        for q in CHUNKS:
            to_columns(Q, q)

    def chunk(slot, q, first=0, count=SIDE):
        return slab(slot, lax.rem(place[0] + q, SIDE) * SIDE + first, count)

    def chunk_wait(kind, q):
        arrived_tiles = pl.ds(0, (SIDE - 1 if q == 0 else SIDE) * own_tiles)
        await_bytes((col_k if kind == Q else col[kind]).at[arrived_tiles], m_recv.at[kind, q])

    def across(kind, slot, q):
        ref = col[kind].at[chunk(slot, q)]
        remote(ref, ref, c_send.at[kind], c_recv.at[kind], device(0, 0, 1))

    def around(kind, q, rows):
        ref = col[kind].at[rows]
        for n, along in enumerate((1, SIDE - 1)):
            remote(ref, ref, x_send.at[kind], x_recv.at[kind, n, q], beside(along))

    def early(kind):
        around(kind, 0, slab(x, here, 1))

    def direct(kind, q):
        chunk_wait(kind, q)
        if kind == K and q == 0:
            for dy in (1, 3, 2):
                around(kind, q, slab(x, place[0] * SIDE + lax.rem(place[1] + dy, SIDE), 1))
        else:
            around(kind, q, chunk(x, q))
        across(kind, x, q)

    def pass_on(kind, q):
        for n, along in enumerate((1, SIDE - 1)):
            slot = lax.rem(x + SIDE - along, SIDE)
            await_bytes(col[kind].at[chunk(slot, q)], x_recv.at[kind, n, q])
            ref = col[kind].at[chunk(slot, q, n * (SIDE // 2), SIDE // 2)]
            remote(ref, ref, x_send.at[kind], x_recv.at[kind, 2 + n, q], beside(along))
            across(kind, slot, q)

    def finish(kind, q):
        slot = lax.rem(x + SIDE // 2, SIDE)
        for n in (0, 1):
            ref = col[kind].at[chunk(slot, q, n * (SIDE // 2), SIDE // 2)]
            await_bytes(ref, x_recv.at[kind, 2 + n, q])
        across(kind, slot, q)

    def complete(kind):
        await_bytes(col[kind].at[slab(0, 0, n_head * COLUMNS, 1 - core)], c_recv.at[kind])
        if kind == K:
            for q in CHUNKS:
                chunk_wait(Q, q)

    lane = lax.broadcasted_iota(jnp.int32, (1, TILE), 1)

    def key_bias(row):
        return jnp.concatenate(
            [jnp.where(lane < look[3, e, row], 0.0, MASKED) for e in range(slots)], axis=1
        )

    def folded_bias(row):
        parts = []
        for e in range(0, slots, 2):
            limit = jnp.where(lane < HALF, look[3, e, row], look[3, e + 1, row])
            for first in (0, HALF):
                parts.append(jnp.where(lane % HALF + first < limit, 0.0, MASKED))
        return jnp.concatenate(parts, axis=1)

    def folded_keys(row):
        parts = []
        for e in range(0, slots, 2):
            pair = [col_k[look[0, e + n, row]] for n in (0, 1)]
            parts += [tile[first : first + HALF] for first in (0, HALF) for tile in pair]
        return parts

    def softmax(query, keys, bias):
        scores = lax.dot_general(
            query, jnp.concatenate(keys, axis=0), (((1,), (1,)), ((), ())),
            preferred_element_type=jnp.float32,
        ) + bias
        rows = jnp.exp2(scores - jnp.max(scores, axis=1, keepdims=True))
        return rows.astype(jnp.bfloat16), 1.0 / jnp.sum(rows, axis=1, keepdims=True)

    def col_row(block, part):
        return (block * CORES + core) * span_tiles + x * own_tiles + part

    def weigh(group):
        each = COLUMNS // GROUPS

        @pl.loop(group * each, (group + 1) * each)
        def _(block):
            for part in range(own_tiles):
                row = col_row(block, part)
                rows, inv = softmax(col_q[block, part], folded_keys(row), folded_bias(row))
                weights[block, part] = rows
                inverse[block, part] = inv

    def mix(kind, turn):
        wide = lax.broadcasted_iota(jnp.int32, (TILE, HD), 1)

        def fold(block, part):
            row = col_row(block, part)
            vals = jnp.concatenate([col[kind][look[0, e, row]] for e in range(slots)], axis=0)
            rows = weights[block, part]
            low, high = [
                jnp.dot(
                    jnp.concatenate(
                        [rows[:, m : m + TILE] for m in range(n * TILE, slots * TILE, 2 * TILE)], axis=1
                    ),
                    vals, preferred_element_type=jnp.float32,
                )
                for n in (0, 1)
            ]
            if part == 0:
                both = low + pltpu.roll(high, HALF, 1)
            else:
                both = pltpu.roll(low, HALF, 1) + high
            return both * inverse[block, part]

        @pl.loop(turn * COLUMNS // 2, (turn + 1) * COLUMNS // 2)
        def _(step):
            off = 5 * (step + 1) % COLUMNS
            dz, dy = off // SIDE, off % SIDE
            z, y = lax.rem(place[0] + dz, SIDE), lax.rem(place[1] + dy, SIDE)
            block = z * SIDE + y
            mixed = jnp.where(wide < HALF, fold(block, 0), fold(block, 1)).astype(jnp.bfloat16)
            col_out[kind // W, block] = mixed

            @pl.when(off > 0)
            def _():
                remote(
                    col_out.at[kind // W, block], landed.at[kind // W, here],
                    o_send.at[kind // W], o_recv.at[kind // W],
                    (z * STRIDE[0] + y * STRIDE[1] + core, x),
                )

    def join(_):
        away = landed.at[0, pl.ds(0, COLUMNS - 1)]
        for n in (0, 1):
            await_bytes(away, o_recv.at[n])
            landed[n, here] = col_out[n, here]
        wide = lax.broadcasted_iota(jnp.int32, (TILE, HD), 1)
        for head in range(COLUMNS):
            low, high = [landed[n, head].astype(jnp.float32) for n in (0, 1)]
            cols = slice(head * HD, (head + 1) * HD)
            o_ref[0, :, cols] = jnp.where(wide < HALF, low, pltpu.roll(high, HALF, 1)).astype(jnp.bfloat16)
            o_ref[1, :, cols] = jnp.where(wide < HALF, pltpu.roll(low, HALF, 1), high).astype(jnp.bfloat16)

    def home(kind):
        return blk_q if kind == Q else ring[kind].at[place[kind]]

    def send(kind):
        for o in (2, 1, 3):
            remote(
                source(kind, COLUMNS + lax.rem(x + o, n_head)), home(kind).at[mine],
                a_send.at[kind], a_recv.at[kind, o - 1], beside(o),
            )
        if kind == Q:
            blk_q[mine] = normalised(Q, rest_head)

    def arrived(kind, o):
        await_bytes(home(kind).at[mine], a_recv.at[kind, o - 1])

    def ring_copy(kind, slot, tiles, n, sem):
        ref = ring[kind].at[slot, tiles]
        along = (1, SIDE - 1)[n]
        remote(ref, ref, r_send.at[kind], r_recv.at[kind, sem], crossing(kind, along, 0, 0))

    def ring_piece(kind, o):
        tiles = pl.ds(lax.rem(x + n_head - o, n_head) * own_tiles, own_tiles)
        for n in (0, 1):
            ring_copy(kind, place[kind], tiles, n, n)

    def own_ring(kind):
        if kind == V:
            own_rest.wait()
        else:
            ring_k[place[K], mine] = normalised(K, rest_head)
        ring_piece(kind, 0)

    def ring_rest(_):
        for o in (1, 3, 2):
            for kind in (V, K):
                arrived(kind, o)
                ring_piece(kind, o)

    def relay(_):
        for kind in (K, V):
            for n in (0, 1):
                await_bytes(ring[kind].at[0], r_recv.at[kind, n])
        for kind in (K, V):
            for n, along in enumerate((1, SIDE - 1)):
                slot = lax.rem(place[kind] + SIDE - along, SIDE)
                ring_copy(kind, slot, pl.ds(n * half, half), n, 2 + n)

    def pick(_):
        to_smem.wait()
        tables_out.wait()
        for kind in (K, V):
            for n in (0, 1):
                await_bytes(ring[kind].at[0, pl.ds(0, half)], r_recv.at[kind, 2 + n])
        for n, (cross, cores) in enumerate(HOPS):
            for kind in (K, V):
                dest = crossing(kind, 0, cross, cores)
                for a in range(SIDE):
                    picked[kind, n, a] = ring[kind][a, wanted[kind * SIDE + a, dest[0] * span_tiles]]
                remote(
                    picked.at[kind, n], bank[kind].at[pl.ds((place[1 - kind] * CORES + core) * SIDE, SIDE)],
                    b_send.at[kind], b_recv.at[kind], dest,
                )
        for kind in (K, V):
            for a in range(SIDE):
                bank[kind][(place[1 - kind] * CORES + core) * SIDE + a] = ring[kind][
                    a, wanted[kind * SIDE + a, s * span_tiles]
                ]

    def attend(_):
        for o in range(1, n_head):
            arrived(Q, o)
        for kind in (K, V):
            await_bytes(bank[kind].at[pl.ds(0, len(HOPS) * SIDE)], b_recv.at[kind])

        @pl.loop(0, span_tiles)
        def _(step):
            i = step
            row = s * span_tiles + i
            mate = i + 1 - 2 * (i % 2)
            keys = [ring_k[place[K], i], ring_k[place[K], mate]]
            vals = [ring_v[place[V], i], ring_v[place[V], mate]]
            for e in range(2, slots):
                keys.append(bank_k[look[1, e, row]])
                vals.append(bank_v[look[2, e, row]])
            rows, inv = softmax(blk_q[i], keys, key_bias(row))
            mixed = jnp.dot(rows, jnp.concatenate(vals, axis=0), preferred_element_type=jnp.float32)
            blk_out[i] = (mixed * inv).astype(jnp.bfloat16)

    def answer(_):
        for o in (2, 1, 3):
            dest = lax.rem(x + o, n_head)
            remote(
                blk_out.at[pl.ds(dest * own_tiles, own_tiles)], o_ref.at[:, :, columns(rest_head)],
                o_send.at[2], o_recv.at[2], beside(o),
            )
        pltpu.make_async_copy(blk_out.at[mine], o_ref.at[:, :, columns(rest_head)], o_own.at[0]).start()

    stages = dict(
        send=send, scale=scale, look_up=look_up, answer=answer, own=own, early=early, spread_k=spread_k, spread_v=spread_v, halve=halve, join=join, spread_q=spread_q,
        own_ring=own_ring, direct=direct, pass_on=pass_on, finish=finish, complete=complete,
        ring_rest=ring_rest, relay=relay, pick=pick, weigh=weigh, attend=attend, mix=mix,
    )
    for name, *args in schedule():
        stages[name](*args)

    away = pl.ds(0, (COLUMNS - 1) * own_tiles)
    aside = blk_q.at[pl.ds(0, span_tiles - own_tiles)]
    for kind in (K, V, Q, W):
        await_bytes((col_k if kind == Q else col[kind]).at[away], m_send.at[kind])
    for kind in (K, V, Q):
        await_bytes(aside, a_send.at[kind])
    for kind in (K, V, W):
        await_bytes(col[kind].at[slab(0, 0, 3 * COLUMNS, 0)], x_send.at[kind])
        await_bytes(col[kind].at[slab(0, 0, n_head * COLUMNS, 0)], c_send.at[kind])
    for kind in (K, V):
        await_bytes(ring_k.at[pl.ds(0, 3)], r_send.at[kind])
        await_bytes(picked.at[kind], b_send.at[kind])
    for n in (0, 1):
        await_bytes(landed.at[0, pl.ds(0, COLUMNS - 1)], o_send.at[n])
    await_bytes(aside, o_send.at[2])
    await_bytes(aside, o_recv.at[2])
    pltpu.make_async_copy(blk_out.at[mine], o_ref.at[:, :, columns(rest_head)], o_own.at[0]).wait()


def on_device(queries, keys, values, gain_q, gain_k, key_tiles, tile_counts, tile_valid):
    n_head = lax.axis_size("head")
    rows, width = queries.shape
    own_tiles = rows // TILE
    span_tiles = own_tiles * n_head
    heads = width // HD
    tiles, slots = key_tiles.shape
    listed = key_tiles.T

    hbm = pl.BlockSpec(memory_space=pl.ANY)
    shape = (own_tiles, TILE, width)
    dma = pltpu.SemaphoreType.DMA

    def buffer(*lead, tail=(TILE, HD), kind=jnp.bfloat16):
        return pltpu.VMEM((*lead, *tail), kind)

    out = pl.pallas_call(
        functools.partial(kernel, n_head),
        out_shape=pltpu.VMEM(shape, jnp.bfloat16),
        in_specs=[hbm] * 8,
        out_specs=pl.BlockSpec(memory_space=pltpu.VMEM),
        scratch_shapes=[
            pltpu.SMEM((tiles,), jnp.int32),
            pltpu.VMEM((width,), jnp.float32),
            pltpu.VMEM((width,), jnp.float32),
            pltpu.VMEM((slots, tiles), jnp.int32),
            pltpu.VMEM((tiles,), jnp.int32),
            pltpu.SemaphoreType.DMA((5,)),
            pltpu.VMEM(shape, jnp.bfloat16),
            pltpu.VMEM(shape, jnp.bfloat16),
            pltpu.VMEM(shape, jnp.bfloat16),
            buffer(heads, own_tiles),
            buffer(heads, own_tiles),
            buffer(2, COLUMNS, own_tiles, tail=(HALF, HD)),
            pltpu.VMEM((2 * SIDE, tiles), jnp.int32),
            pltpu.SMEM((2 * SIDE, tiles), jnp.int32),
            pltpu.VMEM((4, slots, tiles), jnp.int32),
            pltpu.SMEM((4, slots, tiles), jnp.int32),
            buffer(tiles),
            buffer(tiles, tail=(HALF, HD)),
            buffer(tiles, tail=(HALF, HD)),
            buffer(COLUMNS, own_tiles),
            buffer(2, COLUMNS),
            buffer(2, COLUMNS),
            buffer(COLUMNS, own_tiles, tail=(TILE, slots * TILE)),
            buffer(COLUMNS, own_tiles, tail=(TILE, 1), kind=jnp.float32),
            buffer(SIDE, span_tiles),
            buffer(SIDE, span_tiles),
            buffer(SIDE * CORES * SIDE),
            buffer(SIDE * CORES * SIDE),
            buffer(span_tiles),
            buffer(2, len(HOPS), SIDE),
            buffer(span_tiles),
            dma((4,)),
            dma((2,)),
            dma((4,)),
            dma((4, SIDE)),
            dma((4,)),
            dma((4, 4, SIDE)),
            dma((4,)),
            dma((4,)),
            dma((3,)),
            dma((3, n_head - 1)),
            dma((2,)),
            dma((2, 4)),
            dma((2,)),
            dma((2,)),
            dma((3,)),
            dma((3,)),
            dma((1,)),
        ],
        compiler_params=pltpu.CompilerParams(
            collective_id=0, has_side_effects=True, vmem_limit_bytes=58 << 20
        ),
    )(
        tile_valid,
        queries.reshape(shape), keys.reshape(shape), values.reshape(shape),
        gain_q, gain_k, listed, tile_counts,
    )
    return out.reshape(rows, width)


def solution(mesh):
    placed = P(("seq", "head"), None)
    return jax.shard_map(
        on_device,
        mesh=mesh,
        in_specs=(placed, placed, placed, P(), P(), P(), P(), P()),
        out_specs=placed,
        check_vma=False,
    )
```

```python
import functools
import math

import jax
import jax.numpy as jnp
from jax import lax
from jax.experimental import pallas as pl
from jax.experimental.pallas import tpu as pltpu
from jax.sharding import PartitionSpec as P

HD = 128
TILE = 128
EPS = 1e-06
MASKED = -1e30
MESH = pl.DeviceIdType.MESH
LOG2E = math.log2(math.e)
SIDE = 4
CORES = 2
STRIDE = (SIDE * CORES, CORES)
COLUMNS = SIDE * SIDE
HOPS = ((2, 0), (2, 1), (1, 0), (3, 0), (1, 1), (3, 1), (0, 1))
CHUNKS = (0, 1, 3, 2)
GROUPS = 8
K, V, Q, W = 0, 1, 2, 3
HALF = HD // 2


def schedule():
    return (
        [("send", V), ("scale", K), ("own", K), ("early", K), ("send", K), ("spread_k", 0)]
        + [("own_ring", V), ("own_ring", K), ("look_up", 0)]
        + [("direct", K, q) for q in CHUNKS]
        + [("halve", 0)] + [("spread_v", V, q) for q in CHUNKS]
        + [("pass_on", K, 0), ("ring_rest", 0), ("pass_on", K, 1), ("pass_on", K, 3)]
        + [("scale", Q), ("own", Q), ("spread_q", 0), ("send", Q), ("relay", 0)]
        + [("direct", V, 0), ("pass_on", K, 2), ("direct", V, 1)] + [("spread_v", W, q) for q in CHUNKS]
        + [("finish", K, 0), ("pick", 0), ("finish", K, 1)]
        + [("direct", V, 3), ("finish", K, 3), ("direct", V, 2), ("finish", K, 2)]
        + [("pass_on", V, 0), ("direct", W, 0), ("pass_on", V, 1), ("direct", W, 1)]
        + [("complete", K), ("weigh", 0), ("pass_on", V, 3), ("direct", W, 3), ("weigh", 1), ("weigh", 2)]
        + [("pass_on", V, 2), ("direct", W, 2), ("attend", 0), ("weigh", 3), ("finish", V, 0), ("finish", V, 1)]
        + [("pass_on", W, 0), ("weigh", 4), ("finish", V, 3), ("weigh", 5), ("finish", V, 2)]
        + [("pass_on", W, 1), ("weigh", 6), ("pass_on", W, 3), ("weigh", 7), ("pass_on", W, 2), ("answer", 0)]
        + [("complete", V), ("mix", V, 0), ("finish", W, 0), ("mix", V, 1)]
        + [("finish", W, 1), ("finish", W, 3), ("finish", W, 2)]
        + [("complete", W), ("mix", W, 0), ("mix", W, 1), ("join", 0)]
    )


def row_scale(rows_ref, width):
    total = jnp.zeros((rows_ref.shape[0], TILE, HD), jnp.float32)
    for g in range(width // HD):
        part = rows_ref[:, :, g * HD : (g + 1) * HD].astype(jnp.float32)
        total = total + part * part
    return lax.rsqrt(jnp.sum(total, axis=-1, keepdims=True) / width + EPS)


def find_tables(s, place, span_tiles, own_tiles, last_valid, listed_rows, count_row, found, tables):
    slots, tiles = listed_rows.shape
    used = lax.broadcasted_iota(jnp.int32, (slots, tiles), 0) < count_row[...][None]
    listed = jnp.where(used, listed_rows[...], -1)
    span_bits = span_tiles.bit_length() - 1
    owner = listed >> span_bits
    tile = listed & (span_tiles - 1)
    for kind in (K, V):
        for a in range(SIDE):
            source = s + (a - place[kind]) * STRIDE[kind]
            best = jnp.max(jnp.where(owner == source, tile, 0), axis=0, keepdims=True)
            found[pl.ds(kind * SIDE + a, 1), :] = best
    every = listed_rows[...]
    spread = every & (tiles - 1)
    z, y, c = spread >> (span_bits + 3), (spread >> (span_bits + 1)) & 3, (spread >> span_bits) & 1
    own_bits = own_tiles.bit_length() - 1
    column = (c * (span_tiles // own_tiles) + ((spread & (span_tiles - 1)) >> own_bits)) * COLUMNS + z * SIDE + y
    tables[0] = column * own_tiles + (spread & (own_tiles - 1))
    tables[1] = (y * CORES + c) * SIDE + z
    tables[2] = (z * CORES + c) * SIDE + y
    tables[3] = jnp.where(used, jnp.where(every == tiles - 1, last_valid, TILE), 0)
    best = found[...]
    for step in (1, 2, 4):
        best = jnp.maximum(best, pltpu.roll(best, tiles - step, 1))
    found[...] = best


def kernel(
    n_head,
    valid_hbm, q_hbm, k_hbm, v_hbm, gain_q_hbm, gain_k_hbm, listed_hbm, count_hbm,
    o_ref,
    valid, gain_q, gain_k, listed_rows, count_row, small_sem,
    q_in, k_in, v_in, q_norm, k_norm, v_half, found, wanted, tables, look,
    col_k, col_v, col_w, col_q, col_out, landed, weights, inverse,
    ring_k, ring_v, bank_k, bank_v, blk_q, picked, blk_out,
    in_sem, own_sem, m_send, m_recv, x_send, x_recv, c_send, c_recv,
    a_send, a_recv, r_send, r_recv, b_send, b_recv, o_send, o_recv, o_own,
):
    s = lax.axis_index("seq")
    x = lax.axis_index("head")
    place = (s // STRIDE[0], s // STRIDE[1] % SIDE)
    core = s % CORES
    here = place[0] * SIDE + place[1]
    own_tiles = q_hbm.shape[0]
    span_tiles = own_tiles * n_head
    half = span_tiles // 2
    width = q_hbm.shape[2]
    slots, tiles = listed_rows.shape
    mine = pl.ds(x * own_tiles, own_tiles)

    def slab(slot, first, count, lane=core):
        return pl.ds(((lane * n_head + slot) * COLUMNS + first) * own_tiles, count * own_tiles)

    raw = (k_in, None, q_in)
    norm = (k_norm, None, q_norm)
    gain = (gain_k, None, gain_q)
    col = (col_k, col_v, col_q, col_w)
    ring = (ring_k, ring_v)
    bank = (bank_k, bank_v)
    scales = {}

    def device(dz, dy, cores):
        z = lax.rem(place[0] + dz, SIDE)
        y = lax.rem(place[1] + dy, SIDE)
        return (z * STRIDE[0] + y * STRIDE[1] + lax.rem(core + cores, CORES), x)

    def crossing(kind, along, cross, cores):
        return device(along, cross, cores) if kind == K else device(cross, along, cores)

    def beside(o):
        return (s, lax.rem(x + o, n_head))

    def columns(head):
        return pl.ds(pl.multiple_of(head * HD, HD), HD)

    def remote(src, dst, send_sem, recv_sem, dest):
        pltpu.make_async_remote_copy(
            src_ref=src, dst_ref=dst, send_sem=send_sem, recv_sem=recv_sem,
            device_id=dest, device_id_type=MESH,
        ).start()

    def await_bytes(ref, sem):
        pltpu.make_async_copy(ref, ref, sem).wait()

    load_k = pltpu.make_async_copy(k_hbm, k_in, in_sem.at[0])
    load_k.start()
    barrier = pltpu.get_barrier_semaphore()
    friends = [beside(o) for o in range(1, n_head)]
    friends += [device(dz, dy, 0) for dz in range(SIDE) for dy in range(SIDE) if dz + dy]
    friends += [device(0, dy, 1) for dy in range(SIDE)] + [device(dz, 0, 1) for dz in range(1, SIDE)]
    for friend in friends:
        pl.semaphore_signal(barrier, inc=1, device_id=friend, device_id_type=MESH)
    small = [
        pltpu.make_async_copy(src, dst, small_sem.at[n])
        for n, (src, dst) in enumerate((
            (gain_k_hbm, gain_k), (listed_hbm, listed_rows), (count_hbm, count_row),
            (valid_hbm, valid), (gain_q_hbm, gain_q),
        ))
    ]
    for copy in small:
        copy.start()
    load_q = pltpu.make_async_copy(q_hbm, q_in, in_sem.at[1])
    load_q.start()
    rest_head = COLUMNS + x
    own_rest = pltpu.make_async_copy(
        v_hbm.at[:, :, columns(rest_head)], ring_v.at[place[1], mine], own_sem.at[0]
    )
    load_v = pltpu.make_async_copy(v_hbm, v_in, own_sem.at[1])
    own_rest.start()
    load_v.start()

    pl.semaphore_wait(barrier, len(friends))

    to_smem = pltpu.make_async_copy(found, wanted, in_sem.at[2])
    tables_out = pltpu.make_async_copy(tables, look, in_sem.at[3])

    def look_up(_):
        for copy in small[1:4]:
            copy.wait()
        find_tables(
            s, place, span_tiles, own_tiles, valid[tiles - 1], listed_rows, count_row, found, tables
        )
        to_smem.start()
        tables_out.start()

    def scale(kind):
        (load_k if kind == K else load_q).wait()
        small[0 if kind == K else 4].wait()
        scales[kind] = row_scale(raw[kind], width)
        if kind == Q:
            scales[kind] = scales[kind] * (HD**-0.5 * LOG2E)

    def normalised(kind, head):
        cols = columns(head)
        rows = raw[kind][:, :, cols].astype(jnp.float32)
        return (rows * scales[kind] * gain[kind][cols][None, None]).astype(jnp.bfloat16)

    def source(kind, head):
        if kind == V:
            return v_hbm.at[:, :, columns(head)]
        norm[kind][head] = normalised(kind, head)
        return norm[kind].at[head]

    def to_columns(kind, q):
        dz = (SIDE - q) % SIDE
        for dy in CHUNKS:
            if dz + dy:
                z, y = lax.rem(place[0] + dz, SIDE), lax.rem(place[1] + dy, SIDE)
                landing = col_q.at[here] if kind == Q else col[kind].at[slab(x, here, 1)]
                head = z * SIDE + y
                part = v_half.at[kind // W, head] if kind in (V, W) else source(kind, head)
                remote(
                    part, landing, m_send.at[kind],
                    m_recv.at[kind, q], device(dz, dy, 0),
                )

    def own(kind):
        if kind == K:
            col_k[slab(x, here, 1)] = normalised(K, here)
        else:
            col_q[here] = normalised(Q, here)

    def spread_k(_):
        for q in CHUNKS:
            to_columns(K, q)

    def halve(_):
        load_v.wait()
        shape = (2 * HD, 2 * HD)
        i, j = lax.broadcasted_iota(jnp.int32, shape, 0), lax.broadcasted_iota(jnp.int32, shape, 1)
        target = i % HALF + HALF * (i // HD) + HD * (i // HALF % 2)
        mover = jnp.where(j == target, 1.0, 0.0).astype(jnp.bfloat16)
        for head in range(COLUMNS):
            rows = v_in[:, :, head * HD : (head + 1) * HD]
            rows = jnp.concatenate([rows[:, :HALF], rows[:, HALF:]], axis=2).reshape(own_tiles * HALF, 2 * HD)
            moved = jnp.dot(rows, mover, preferred_element_type=jnp.float32).astype(jnp.bfloat16)
            for n in (0, 1):
                v_half[n, head] = moved[:, n * HD : (n + 1) * HD].reshape(own_tiles, HALF, HD)
        for n, ref in enumerate((col_v, col_w)):
            ref[slab(x, here, 1)] = v_half[n, here]

    def spread_v(kind, q):
        to_columns(kind, q)

    def spread_q(_):
        for q in CHUNKS:
            to_columns(Q, q)

    def chunk(slot, q, first=0, count=SIDE):
        return slab(slot, lax.rem(place[0] + q, SIDE) * SIDE + first, count)

    def chunk_wait(kind, q):
        arrived_tiles = pl.ds(0, (SIDE - 1 if q == 0 else SIDE) * own_tiles)
        await_bytes((col_k if kind == Q else col[kind]).at[arrived_tiles], m_recv.at[kind, q])

    def across(kind, slot, q):
        ref = col[kind].at[chunk(slot, q)]
        remote(ref, ref, c_send.at[kind], c_recv.at[kind], device(0, 0, 1))

    def around(kind, q, rows):
        ref = col[kind].at[rows]
        for n, along in enumerate((1, SIDE - 1)):
            remote(ref, ref, x_send.at[kind], x_recv.at[kind, n, q], beside(along))

    def early(kind):
        around(kind, 0, slab(x, here, 1))

    def direct(kind, q):
        chunk_wait(kind, q)
        if kind == K and q == 0:
            for dy in (1, 3, 2):
                around(kind, q, slab(x, place[0] * SIDE + lax.rem(place[1] + dy, SIDE), 1))
        else:
            around(kind, q, chunk(x, q))
        across(kind, x, q)

    def pass_on(kind, q):
        for n, along in enumerate((1, SIDE - 1)):
            slot = lax.rem(x + SIDE - along, SIDE)
            await_bytes(col[kind].at[chunk(slot, q)], x_recv.at[kind, n, q])
            ref = col[kind].at[chunk(slot, q, n * (SIDE // 2), SIDE // 2)]
            remote(ref, ref, x_send.at[kind], x_recv.at[kind, 2 + n, q], beside(along))
            across(kind, slot, q)

    def finish(kind, q):
        slot = lax.rem(x + SIDE // 2, SIDE)
        for n in (0, 1):
            ref = col[kind].at[chunk(slot, q, n * (SIDE // 2), SIDE // 2)]
            await_bytes(ref, x_recv.at[kind, 2 + n, q])
        across(kind, slot, q)

    def complete(kind):
        await_bytes(col[kind].at[slab(0, 0, n_head * COLUMNS, 1 - core)], c_recv.at[kind])
        if kind == K:
            for q in CHUNKS:
                chunk_wait(Q, q)

    lane = lax.broadcasted_iota(jnp.int32, (1, TILE), 1)

    def key_bias(row):
        return jnp.concatenate(
            [jnp.where(lane < look[3, e, row], 0.0, MASKED) for e in range(slots)], axis=1
        )

    def folded_bias(row):
        parts = []
        for e in range(0, slots, 2):
            limit = jnp.where(lane < HALF, look[3, e, row], look[3, e + 1, row])
            for first in (0, HALF):
                parts.append(jnp.where(lane % HALF + first < limit, 0.0, MASKED))
        return jnp.concatenate(parts, axis=1)

    def folded_keys(row):
        parts = []
        for e in range(0, slots, 2):
            pair = [col_k[look[0, e + n, row]] for n in (0, 1)]
            parts += [tile[first : first + HALF] for first in (0, HALF) for tile in pair]
        return parts

    def softmax(query, keys, bias):
        scores = lax.dot_general(
            query, jnp.concatenate(keys, axis=0), (((1,), (1,)), ((), ())),
            preferred_element_type=jnp.float32,
        ) + bias
        rows = jnp.exp2(scores - jnp.max(scores, axis=1, keepdims=True))
        return rows.astype(jnp.bfloat16), 1.0 / jnp.sum(rows, axis=1, keepdims=True)

    def col_row(block, part):
        return (block * CORES + core) * span_tiles + x * own_tiles + part

    def weigh(group):
        each = COLUMNS // GROUPS

        @pl.loop(group * each, (group + 1) * each)
        def _(block):
            for part in range(own_tiles):
                row = col_row(block, part)
                rows, inv = softmax(col_q[block, part], folded_keys(row), folded_bias(row))
                weights[block, part] = rows
                inverse[block, part] = inv

    def mix(kind, turn):
        wide = lax.broadcasted_iota(jnp.int32, (TILE, HD), 1)

        def fold(block, part):
            row = col_row(block, part)
            vals = jnp.concatenate([col[kind][look[0, e, row]] for e in range(slots)], axis=0)
            rows = weights[block, part]
            low, high = [
                jnp.dot(
                    jnp.concatenate(
                        [rows[:, m : m + TILE] for m in range(n * TILE, slots * TILE, 2 * TILE)], axis=1
                    ),
                    vals, preferred_element_type=jnp.float32,
                )
                for n in (0, 1)
            ]
            if part == 0:
                both = low + pltpu.roll(high, HALF, 1)
            else:
                both = pltpu.roll(low, HALF, 1) + high
            return both * inverse[block, part]

        @pl.loop(turn * COLUMNS // 2, (turn + 1) * COLUMNS // 2)
        def _(step):
            off = 5 * (step + 1) % COLUMNS
            dz, dy = off // SIDE, off % SIDE
            z, y = lax.rem(place[0] + dz, SIDE), lax.rem(place[1] + dy, SIDE)
            block = z * SIDE + y
            mixed = jnp.where(wide < HALF, fold(block, 0), fold(block, 1)).astype(jnp.bfloat16)
            col_out[kind // W, block] = mixed

            @pl.when(off > 0)
            def _():
                remote(
                    col_out.at[kind // W, block], landed.at[kind // W, here],
                    o_send.at[kind // W], o_recv.at[kind // W],
                    (z * STRIDE[0] + y * STRIDE[1] + core, x),
                )

    def join(_):
        away = landed.at[0, pl.ds(0, COLUMNS - 1)]
        for n in (0, 1):
            await_bytes(away, o_recv.at[n])
            landed[n, here] = col_out[n, here]
        wide = lax.broadcasted_iota(jnp.int32, (TILE, HD), 1)
        for head in range(COLUMNS):
            low, high = [landed[n, head].astype(jnp.float32) for n in (0, 1)]
            cols = slice(head * HD, (head + 1) * HD)
            o_ref[0, :, cols] = jnp.where(wide < HALF, low, pltpu.roll(high, HALF, 1)).astype(jnp.bfloat16)
            o_ref[1, :, cols] = jnp.where(wide < HALF, pltpu.roll(low, HALF, 1), high).astype(jnp.bfloat16)

    def home(kind):
        return blk_q if kind == Q else ring[kind].at[place[kind]]

    def send(kind):
        for o in (2, 1, 3):
            remote(
                source(kind, COLUMNS + lax.rem(x + o, n_head)), home(kind).at[mine],
                a_send.at[kind], a_recv.at[kind, o - 1], beside(o),
            )
        if kind == Q:
            blk_q[mine] = normalised(Q, rest_head)

    def arrived(kind, o):
        await_bytes(home(kind).at[mine], a_recv.at[kind, o - 1])

    def ring_copy(kind, slot, tiles, n, sem):
        ref = ring[kind].at[slot, tiles]
        along = (1, SIDE - 1)[n]
        remote(ref, ref, r_send.at[kind], r_recv.at[kind, sem], crossing(kind, along, 0, 0))

    def ring_piece(kind, o):
        tiles = pl.ds(lax.rem(x + n_head - o, n_head) * own_tiles, own_tiles)
        for n in (0, 1):
            ring_copy(kind, place[kind], tiles, n, n)

    def own_ring(kind):
        if kind == V:
            own_rest.wait()
        else:
            ring_k[place[K], mine] = normalised(K, rest_head)
        ring_piece(kind, 0)

    def ring_rest(_):
        for o in (1, 3, 2):
            for kind in (V, K):
                arrived(kind, o)
                ring_piece(kind, o)

    def relay(_):
        for kind in (K, V):
            for n in (0, 1):
                await_bytes(ring[kind].at[0], r_recv.at[kind, n])
        for kind in (K, V):
            for n, along in enumerate((1, SIDE - 1)):
                slot = lax.rem(place[kind] + SIDE - along, SIDE)
                ring_copy(kind, slot, pl.ds(n * half, half), n, 2 + n)

    def pick(_):
        to_smem.wait()
        tables_out.wait()
        for kind in (K, V):
            for n in (0, 1):
                await_bytes(ring[kind].at[0, pl.ds(0, half)], r_recv.at[kind, 2 + n])
        for n, (cross, cores) in enumerate(HOPS):
            for kind in (K, V):
                dest = crossing(kind, 0, cross, cores)
                for a in range(SIDE):
                    picked[kind, n, a] = ring[kind][a, wanted[kind * SIDE + a, dest[0] * span_tiles]]
                remote(
                    picked.at[kind, n], bank[kind].at[pl.ds((place[1 - kind] * CORES + core) * SIDE, SIDE)],
                    b_send.at[kind], b_recv.at[kind], dest,
                )
        for kind in (K, V):
            for a in range(SIDE):
                bank[kind][(place[1 - kind] * CORES + core) * SIDE + a] = ring[kind][
                    a, wanted[kind * SIDE + a, s * span_tiles]
                ]

    def attend(_):
        for o in range(1, n_head):
            arrived(Q, o)
        for kind in (K, V):
            await_bytes(bank[kind].at[pl.ds(0, len(HOPS) * SIDE)], b_recv.at[kind])

        @pl.loop(0, span_tiles)
        def _(step):
            i = step
            row = s * span_tiles + i
            mate = i + 1 - 2 * (i % 2)
            keys = [ring_k[place[K], i], ring_k[place[K], mate]]
            vals = [ring_v[place[V], i], ring_v[place[V], mate]]
            for e in range(2, slots):
                keys.append(bank_k[look[1, e, row]])
                vals.append(bank_v[look[2, e, row]])
            rows, inv = softmax(blk_q[i], keys, key_bias(row))
            mixed = jnp.dot(rows, jnp.concatenate(vals, axis=0), preferred_element_type=jnp.float32)
            blk_out[i] = (mixed * inv).astype(jnp.bfloat16)

    def answer(_):
        for o in (2, 1, 3):
            dest = lax.rem(x + o, n_head)
            remote(
                blk_out.at[pl.ds(dest * own_tiles, own_tiles)], o_ref.at[:, :, columns(rest_head)],
                o_send.at[2], o_recv.at[2], beside(o),
            )
        pltpu.make_async_copy(blk_out.at[mine], o_ref.at[:, :, columns(rest_head)], o_own.at[0]).start()

    stages = dict(
        send=send, scale=scale, look_up=look_up, answer=answer, own=own, early=early, spread_k=spread_k, spread_v=spread_v, halve=halve, join=join, spread_q=spread_q,
        own_ring=own_ring, direct=direct, pass_on=pass_on, finish=finish, complete=complete,
        ring_rest=ring_rest, relay=relay, pick=pick, weigh=weigh, attend=attend, mix=mix,
    )
    for name, *args in schedule():
        stages[name](*args)

    away = pl.ds(0, (COLUMNS - 1) * own_tiles)
    aside = blk_q.at[pl.ds(0, span_tiles - own_tiles)]
    for kind in (K, V, Q, W):
        await_bytes((col_k if kind == Q else col[kind]).at[away], m_send.at[kind])
    for kind in (K, V, Q):
        await_bytes(aside, a_send.at[kind])
    for kind in (K, V, W):
        await_bytes(col[kind].at[slab(0, 0, 3 * COLUMNS, 0)], x_send.at[kind])
        await_bytes(col[kind].at[slab(0, 0, n_head * COLUMNS, 0)], c_send.at[kind])
    for kind in (K, V):
        await_bytes(ring_k.at[pl.ds(0, 3)], r_send.at[kind])
        await_bytes(picked.at[kind], b_send.at[kind])
    for n in (0, 1):
        await_bytes(landed.at[0, pl.ds(0, COLUMNS - 1)], o_send.at[n])
    await_bytes(aside, o_send.at[2])
    await_bytes(aside, o_recv.at[2])
    pltpu.make_async_copy(blk_out.at[mine], o_ref.at[:, :, columns(rest_head)], o_own.at[0]).wait()


def on_device(queries, keys, values, gain_q, gain_k, key_tiles, tile_counts, tile_valid):
    n_head = lax.axis_size("head")
    rows, width = queries.shape
    own_tiles = rows // TILE
    span_tiles = own_tiles * n_head
    heads = width // HD
    tiles, slots = key_tiles.shape
    listed = key_tiles.T

    hbm = pl.BlockSpec(memory_space=pl.ANY)
    shape = (own_tiles, TILE, width)
    dma = pltpu.SemaphoreType.DMA

    def buffer(*lead, tail=(TILE, HD), kind=jnp.bfloat16):
        return pltpu.VMEM((*lead, *tail), kind)

    out = pl.pallas_call(
        functools.partial(kernel, n_head),
        out_shape=pltpu.VMEM(shape, jnp.bfloat16),
        in_specs=[hbm] * 8,
        out_specs=pl.BlockSpec(memory_space=pltpu.VMEM),
        scratch_shapes=[
            pltpu.SMEM((tiles,), jnp.int32),
            pltpu.VMEM((width,), jnp.float32),
            pltpu.VMEM((width,), jnp.float32),
            pltpu.VMEM((slots, tiles), jnp.int32),
            pltpu.VMEM((tiles,), jnp.int32),
            pltpu.SemaphoreType.DMA((5,)),
            pltpu.VMEM(shape, jnp.bfloat16),
            pltpu.VMEM(shape, jnp.bfloat16),
            pltpu.VMEM(shape, jnp.bfloat16),
            buffer(heads, own_tiles),
            buffer(heads, own_tiles),
            buffer(2, COLUMNS, own_tiles, tail=(HALF, HD)),
            pltpu.VMEM((2 * SIDE, tiles), jnp.int32),
            pltpu.SMEM((2 * SIDE, tiles), jnp.int32),
            pltpu.VMEM((4, slots, tiles), jnp.int32),
            pltpu.SMEM((4, slots, tiles), jnp.int32),
            buffer(tiles),
            buffer(tiles, tail=(HALF, HD)),
            buffer(tiles, tail=(HALF, HD)),
            buffer(COLUMNS, own_tiles),
            buffer(2, COLUMNS),
            buffer(2, COLUMNS),
            buffer(COLUMNS, own_tiles, tail=(TILE, slots * TILE)),
            buffer(COLUMNS, own_tiles, tail=(TILE, 1), kind=jnp.float32),
            buffer(SIDE, span_tiles),
            buffer(SIDE, span_tiles),
            buffer(SIDE * CORES * SIDE),
            buffer(SIDE * CORES * SIDE),
            buffer(span_tiles),
            buffer(2, len(HOPS), SIDE),
            buffer(span_tiles),
            dma((4,)),
            dma((2,)),
            dma((4,)),
            dma((4, SIDE)),
            dma((4,)),
            dma((4, 4, SIDE)),
            dma((4,)),
            dma((4,)),
            dma((3,)),
            dma((3, n_head - 1)),
            dma((2,)),
            dma((2, 4)),
            dma((2,)),
            dma((2,)),
            dma((3,)),
            dma((3,)),
            dma((1,)),
        ],
        compiler_params=pltpu.CompilerParams(
            collective_id=0, has_side_effects=True, vmem_limit_bytes=58 << 20
        ),
    )(
        tile_valid,
        queries.reshape(shape), keys.reshape(shape), values.reshape(shape),
        gain_q, gain_k, listed, tile_counts,
    )
    return out.reshape(rows, width)


def solution(mesh):
    placed = P(("seq", "head"), None)
    return jax.shard_map(
        on_device,
        mesh=mesh,
        in_specs=(placed, placed, placed, P(), P(), P(), P(), P()),
        out_specs=placed,
        check_vma=False,
    )
```

```python
import functools
import math

import jax
import jax.numpy as jnp
from jax import lax
from jax.experimental import pallas as pl
from jax.experimental.pallas import tpu as pltpu
from jax.sharding import PartitionSpec as P

HD = 128
TILE = 128
EPS = 1e-06
MASKED = -1e30
MESH = pl.DeviceIdType.MESH
LOG2E = math.log2(math.e)
SIDE = 4
CORES = 2
STRIDE = (SIDE * CORES, CORES)
COLUMNS = SIDE * SIDE
HOPS = ((2, 0), (2, 1), (1, 0), (3, 0), (1, 1), (3, 1), (0, 1))
CHUNKS = (0, 1, 3, 2)
GROUPS = 8
TURNS = 4
K, V, Q, W = 0, 1, 2, 3
HALF = HD // 2


def schedule():
    return (
        [("send", V), ("scale", K), ("own", K), ("early", K), ("send", K), ("spread_k", 0)]
        + [("own_ring", V), ("own_ring", K), ("look_up", 0)]
        + [("direct", K, q) for q in CHUNKS]
        + [("halve", 0)] + [("spread_v", V, q) for q in CHUNKS]
        + [("pass_on", K, 0), ("ring_rest", 0), ("pass_on", K, 1), ("pass_on", K, 3)]
        + [("scale", Q), ("own", Q), ("spread_q", 0), ("send", Q), ("relay", 0)]
        + [("direct", V, 0), ("pass_on", K, 2), ("direct", V, 1)] + [("spread_v", W, q) for q in CHUNKS]
        + [("finish", K, 0), ("pick", 0), ("finish", K, 1)]
        + [("direct", V, 3), ("finish", K, 3), ("direct", V, 2), ("finish", K, 2)]
        + [("pass_on", V, 0), ("direct", W, 0), ("pass_on", V, 1), ("direct", W, 1)]
        + [("complete", K), ("weigh", 0), ("pass_on", V, 3), ("direct", W, 3), ("weigh", 1), ("weigh", 2)]
        + [("pass_on", V, 2), ("direct", W, 2), ("attend", 0), ("weigh", 3), ("finish", V, 0), ("finish", V, 1)]
        + [("pass_on", W, 0), ("weigh", 4), ("finish", V, 3), ("weigh", 5), ("finish", V, 2)]
        + [("pass_on", W, 1), ("weigh", 6), ("pass_on", W, 3), ("weigh", 7), ("pass_on", W, 2), ("answer", 0)]
        + [("complete", V), ("mix", V, 0), ("mix", V, 1), ("finish", W, 0), ("mix", V, 2)]
        + [("finish", W, 1), ("mix", V, 3), ("finish", W, 3), ("finish", W, 2)]
        + [("complete", W)] + [("mix", W, turn) for turn in range(TURNS)] + [("join", 0)]
    )


def row_scale(rows_ref, width):
    total = jnp.zeros((rows_ref.shape[0], TILE, HD), jnp.float32)
    for g in range(width // HD):
        part = rows_ref[:, :, g * HD : (g + 1) * HD].astype(jnp.float32)
        total = total + part * part
    return lax.rsqrt(jnp.sum(total, axis=-1, keepdims=True) / width + EPS)


def find_tables(s, place, span_tiles, own_tiles, last_valid, listed_rows, count_row, found, tables):
    slots, tiles = listed_rows.shape
    used = lax.broadcasted_iota(jnp.int32, (slots, tiles), 0) < count_row[...][None]
    listed = jnp.where(used, listed_rows[...], -1)
    span_bits = span_tiles.bit_length() - 1
    owner = listed >> span_bits
    tile = listed & (span_tiles - 1)
    for kind in (K, V):
        for a in range(SIDE):
            source = s + (a - place[kind]) * STRIDE[kind]
            best = jnp.max(jnp.where(owner == source, tile, 0), axis=0, keepdims=True)
            found[pl.ds(kind * SIDE + a, 1), :] = best
    every = listed_rows[...]
    spread = every & (tiles - 1)
    z, y, c = spread >> (span_bits + 3), (spread >> (span_bits + 1)) & 3, (spread >> span_bits) & 1
    own_bits = own_tiles.bit_length() - 1
    column = (c * (span_tiles // own_tiles) + ((spread & (span_tiles - 1)) >> own_bits)) * COLUMNS + z * SIDE + y
    tables[0] = column * own_tiles + (spread & (own_tiles - 1))
    tables[1] = (y * CORES + c) * SIDE + z
    tables[2] = (z * CORES + c) * SIDE + y
    tables[3] = jnp.where(used, jnp.where(every == tiles - 1, last_valid, TILE), 0)
    best = found[...]
    for step in (1, 2, 4):
        best = jnp.maximum(best, pltpu.roll(best, tiles - step, 1))
    found[...] = best


def kernel(
    n_head,
    valid_hbm, q_hbm, k_hbm, v_hbm, gain_q_hbm, gain_k_hbm, listed_hbm, count_hbm,
    o_ref,
    valid, gain_q, gain_k, listed_rows, count_row, small_sem,
    q_in, k_in, v_in, q_norm, k_norm, v_half, found, wanted, tables, look,
    col_k, col_v, col_w, col_q, col_out, landed, weights, inverse,
    ring_k, ring_v, bank_k, bank_v, blk_q, picked, blk_out,
    in_sem, own_sem, m_send, m_recv, x_send, x_recv, c_send, c_recv,
    a_send, a_recv, r_send, r_recv, b_send, b_recv, o_send, o_recv, o_own,
):
    s = lax.axis_index("seq")
    x = lax.axis_index("head")
    place = (s // STRIDE[0], s // STRIDE[1] % SIDE)
    core = s % CORES
    here = place[0] * SIDE + place[1]
    own_tiles = q_hbm.shape[0]
    span_tiles = own_tiles * n_head
    half = span_tiles // 2
    width = q_hbm.shape[2]
    slots, tiles = listed_rows.shape
    mine = pl.ds(x * own_tiles, own_tiles)

    def slab(slot, first, count, lane=core):
        return pl.ds(((lane * n_head + slot) * COLUMNS + first) * own_tiles, count * own_tiles)

    raw = (k_in, None, q_in)
    norm = (k_norm, None, q_norm)
    gain = (gain_k, None, gain_q)
    col = (col_k, col_v, col_q, col_w)
    ring = (ring_k, ring_v)
    bank = (bank_k, bank_v)
    scales = {}

    def device(dz, dy, cores):
        z = lax.rem(place[0] + dz, SIDE)
        y = lax.rem(place[1] + dy, SIDE)
        return (z * STRIDE[0] + y * STRIDE[1] + lax.rem(core + cores, CORES), x)

    def crossing(kind, along, cross, cores):
        return device(along, cross, cores) if kind == K else device(cross, along, cores)

    def beside(o):
        return (s, lax.rem(x + o, n_head))

    def columns(head):
        return pl.ds(pl.multiple_of(head * HD, HD), HD)

    def remote(src, dst, send_sem, recv_sem, dest):
        pltpu.make_async_remote_copy(
            src_ref=src, dst_ref=dst, send_sem=send_sem, recv_sem=recv_sem,
            device_id=dest, device_id_type=MESH,
        ).start()

    def await_bytes(ref, sem):
        pltpu.make_async_copy(ref, ref, sem).wait()

    load_k = pltpu.make_async_copy(k_hbm, k_in, in_sem.at[0])
    load_k.start()
    barrier = pltpu.get_barrier_semaphore()
    friends = [beside(o) for o in range(1, n_head)]
    friends += [device(dz, dy, 0) for dz in range(SIDE) for dy in range(SIDE) if dz + dy]
    friends += [device(0, dy, 1) for dy in range(SIDE)] + [device(dz, 0, 1) for dz in range(1, SIDE)]
    for friend in friends:
        pl.semaphore_signal(barrier, inc=1, device_id=friend, device_id_type=MESH)
    small = [
        pltpu.make_async_copy(src, dst, small_sem.at[n])
        for n, (src, dst) in enumerate((
            (gain_k_hbm, gain_k), (listed_hbm, listed_rows), (count_hbm, count_row),
            (valid_hbm, valid), (gain_q_hbm, gain_q),
        ))
    ]
    for copy in small:
        copy.start()
    load_q = pltpu.make_async_copy(q_hbm, q_in, in_sem.at[1])
    load_q.start()
    rest_head = COLUMNS + x
    own_rest = pltpu.make_async_copy(
        v_hbm.at[:, :, columns(rest_head)], ring_v.at[place[1], mine], own_sem.at[0]
    )
    load_v = pltpu.make_async_copy(v_hbm, v_in, own_sem.at[1])
    own_rest.start()
    load_v.start()

    pl.semaphore_wait(barrier, len(friends))

    to_smem = pltpu.make_async_copy(found, wanted, in_sem.at[2])
    tables_out = pltpu.make_async_copy(tables, look, in_sem.at[3])

    def look_up(_):
        for copy in small[1:4]:
            copy.wait()
        find_tables(
            s, place, span_tiles, own_tiles, valid[tiles - 1], listed_rows, count_row, found, tables
        )
        to_smem.start()
        tables_out.start()

    def scale(kind):
        (load_k if kind == K else load_q).wait()
        small[0 if kind == K else 4].wait()
        scales[kind] = row_scale(raw[kind], width)
        if kind == Q:
            scales[kind] = scales[kind] * (HD**-0.5 * LOG2E)

    def normalised(kind, head):
        cols = columns(head)
        rows = raw[kind][:, :, cols].astype(jnp.float32)
        return (rows * scales[kind] * gain[kind][cols][None, None]).astype(jnp.bfloat16)

    def source(kind, head):
        if kind == V:
            return v_hbm.at[:, :, columns(head)]
        norm[kind][head] = normalised(kind, head)
        return norm[kind].at[head]

    def to_columns(kind, q):
        dz = (SIDE - q) % SIDE
        for dy in CHUNKS:
            if dz + dy:
                z, y = lax.rem(place[0] + dz, SIDE), lax.rem(place[1] + dy, SIDE)
                landing = col_q.at[here] if kind == Q else col[kind].at[slab(x, here, 1)]
                head = z * SIDE + y
                part = v_half.at[kind // W, head] if kind in (V, W) else source(kind, head)
                remote(
                    part, landing, m_send.at[kind],
                    m_recv.at[kind, q], device(dz, dy, 0),
                )

    def own(kind):
        if kind == K:
            col_k[slab(x, here, 1)] = normalised(K, here)
        else:
            col_q[here] = normalised(Q, here)

    def spread_k(_):
        for q in CHUNKS:
            to_columns(K, q)

    def halve(_):
        load_v.wait()
        shape = (2 * HD, 2 * HD)
        i, j = lax.broadcasted_iota(jnp.int32, shape, 0), lax.broadcasted_iota(jnp.int32, shape, 1)
        target = i % HALF + HALF * (i // HD) + HD * (i // HALF % 2)
        mover = jnp.where(j == target, 1.0, 0.0).astype(jnp.bfloat16)
        for head in range(COLUMNS):
            rows = v_in[:, :, head * HD : (head + 1) * HD]
            rows = jnp.concatenate([rows[:, :HALF], rows[:, HALF:]], axis=2).reshape(own_tiles * HALF, 2 * HD)
            moved = jnp.dot(rows, mover, preferred_element_type=jnp.float32).astype(jnp.bfloat16)
            for n in (0, 1):
                v_half[n, head] = moved[:, n * HD : (n + 1) * HD].reshape(own_tiles, HALF, HD)
        for n, ref in enumerate((col_v, col_w)):
            ref[slab(x, here, 1)] = v_half[n, here]

    def spread_v(kind, q):
        to_columns(kind, q)

    def spread_q(_):
        for q in CHUNKS:
            to_columns(Q, q)

    def chunk(slot, q, first=0, count=SIDE):
        return slab(slot, lax.rem(place[0] + q, SIDE) * SIDE + first, count)

    def chunk_wait(kind, q):
        arrived_tiles = pl.ds(0, (SIDE - 1 if q == 0 else SIDE) * own_tiles)
        await_bytes((col_k if kind == Q else col[kind]).at[arrived_tiles], m_recv.at[kind, q])

    def across(kind, slot, q):
        ref = col[kind].at[chunk(slot, q)]
        remote(ref, ref, c_send.at[kind], c_recv.at[kind], device(0, 0, 1))

    def around(kind, q, rows):
        ref = col[kind].at[rows]
        for n, along in enumerate((1, SIDE - 1)):
            remote(ref, ref, x_send.at[kind], x_recv.at[kind, n, q], beside(along))

    def early(kind):
        around(kind, 0, slab(x, here, 1))

    def direct(kind, q):
        chunk_wait(kind, q)
        if kind == K and q == 0:
            for dy in (1, 3, 2):
                around(kind, q, slab(x, place[0] * SIDE + lax.rem(place[1] + dy, SIDE), 1))
        else:
            around(kind, q, chunk(x, q))
        across(kind, x, q)

    def pass_on(kind, q):
        for n, along in enumerate((1, SIDE - 1)):
            slot = lax.rem(x + SIDE - along, SIDE)
            await_bytes(col[kind].at[chunk(slot, q)], x_recv.at[kind, n, q])
            ref = col[kind].at[chunk(slot, q, n * (SIDE // 2), SIDE // 2)]
            remote(ref, ref, x_send.at[kind], x_recv.at[kind, 2 + n, q], beside(along))
            across(kind, slot, q)

    def finish(kind, q):
        slot = lax.rem(x + SIDE // 2, SIDE)
        for n in (0, 1):
            ref = col[kind].at[chunk(slot, q, n * (SIDE // 2), SIDE // 2)]
            await_bytes(ref, x_recv.at[kind, 2 + n, q])
        across(kind, slot, q)

    def complete(kind):
        await_bytes(col[kind].at[slab(0, 0, n_head * COLUMNS, 1 - core)], c_recv.at[kind])
        if kind == K:
            for q in CHUNKS:
                chunk_wait(Q, q)

    lane = lax.broadcasted_iota(jnp.int32, (1, TILE), 1)

    def key_bias(row):
        return jnp.concatenate(
            [jnp.where(lane < look[3, e, row], 0.0, MASKED) for e in range(slots)], axis=1
        )

    def folded_bias(row):
        parts = []
        for e in range(0, slots, 2):
            limit = jnp.where(lane < HALF, look[3, e, row], look[3, e + 1, row])
            for first in (0, HALF):
                parts.append(jnp.where(lane % HALF + first < limit, 0.0, MASKED))
        return jnp.concatenate(parts, axis=1)

    def folded_keys(row):
        parts = []
        for e in range(0, slots, 2):
            pair = [col_k[look[0, e + n, row]] for n in (0, 1)]
            parts += [tile[first : first + HALF] for first in (0, HALF) for tile in pair]
        return parts

    def softmax(query, keys, bias):
        scores = lax.dot_general(
            query, jnp.concatenate(keys, axis=0), (((1,), (1,)), ((), ())),
            preferred_element_type=jnp.float32,
        ) + bias
        rows = jnp.exp2(scores - jnp.max(scores, axis=1, keepdims=True))
        return rows.astype(jnp.bfloat16), 1.0 / jnp.sum(rows, axis=1, keepdims=True)

    def col_row(block, part):
        return (block * CORES + core) * span_tiles + x * own_tiles + part

    def weigh(group):
        each = COLUMNS // GROUPS

        @pl.loop(group * each, (group + 1) * each)
        def _(block):
            for part in range(own_tiles):
                row = col_row(block, part)
                rows, inv = softmax(col_q[block, part], folded_keys(row), folded_bias(row))
                weights[block, part] = rows
                inverse[block, part] = inv

    def mix(kind, turn):
        wide = lax.broadcasted_iota(jnp.int32, (TILE, HD), 1)

        def fold(block, part):
            row = col_row(block, part)
            vals = jnp.concatenate([col[kind][look[0, e, row]] for e in range(slots)], axis=0)
            rows = weights[block, part]
            low, high = [
                jnp.dot(
                    jnp.concatenate(
                        [rows[:, m : m + TILE] for m in range(n * TILE, slots * TILE, 2 * TILE)], axis=1
                    ),
                    vals, preferred_element_type=jnp.float32,
                )
                for n in (0, 1)
            ]
            if part == 0:
                both = low + pltpu.roll(high, HALF, 1)
            else:
                both = pltpu.roll(low, HALF, 1) + high
            return both * inverse[block, part]

        @pl.loop(turn * COLUMNS // TURNS, (turn + 1) * COLUMNS // TURNS)
        def _(step):
            off = 5 * (step + 1) % COLUMNS
            dz, dy = off // SIDE, off % SIDE
            z, y = lax.rem(place[0] + dz, SIDE), lax.rem(place[1] + dy, SIDE)
            block = z * SIDE + y
            mixed = jnp.where(wide < HALF, fold(block, 0), fold(block, 1)).astype(jnp.bfloat16)
            col_out[kind // W, block] = mixed

            @pl.when(off > 0)
            def _():
                remote(
                    col_out.at[kind // W, block], landed.at[kind // W, here],
                    o_send.at[kind // W], o_recv.at[kind // W],
                    (z * STRIDE[0] + y * STRIDE[1] + core, x),
                )

    def join(_):
        away = landed.at[0, pl.ds(0, COLUMNS - 1)]
        for n in (0, 1):
            await_bytes(away, o_recv.at[n])
            landed[n, here] = col_out[n, here]
        wide = lax.broadcasted_iota(jnp.int32, (TILE, HD), 1)
        for head in range(COLUMNS):
            low, high = [landed[n, head].astype(jnp.float32) for n in (0, 1)]
            cols = slice(head * HD, (head + 1) * HD)
            o_ref[0, :, cols] = jnp.where(wide < HALF, low, pltpu.roll(high, HALF, 1)).astype(jnp.bfloat16)
            o_ref[1, :, cols] = jnp.where(wide < HALF, pltpu.roll(low, HALF, 1), high).astype(jnp.bfloat16)

    def home(kind):
        return blk_q if kind == Q else ring[kind].at[place[kind]]

    def send(kind):
        for o in (2, 1, 3):
            remote(
                source(kind, COLUMNS + lax.rem(x + o, n_head)), home(kind).at[mine],
                a_send.at[kind], a_recv.at[kind, o - 1], beside(o),
            )
        if kind == Q:
            blk_q[mine] = normalised(Q, rest_head)

    def arrived(kind, o):
        await_bytes(home(kind).at[mine], a_recv.at[kind, o - 1])

    def ring_copy(kind, slot, tiles, n, sem):
        ref = ring[kind].at[slot, tiles]
        along = (1, SIDE - 1)[n]
        remote(ref, ref, r_send.at[kind], r_recv.at[kind, sem], crossing(kind, along, 0, 0))

    def ring_piece(kind, o):
        tiles = pl.ds(lax.rem(x + n_head - o, n_head) * own_tiles, own_tiles)
        for n in (0, 1):
            ring_copy(kind, place[kind], tiles, n, n)

    def own_ring(kind):
        if kind == V:
            own_rest.wait()
        else:
            ring_k[place[K], mine] = normalised(K, rest_head)
        ring_piece(kind, 0)

    def ring_rest(_):
        for o in (1, 3, 2):
            for kind in (V, K):
                arrived(kind, o)
                ring_piece(kind, o)

    def relay(_):
        for kind in (K, V):
            for n in (0, 1):
                await_bytes(ring[kind].at[0], r_recv.at[kind, n])
        for kind in (K, V):
            for n, along in enumerate((1, SIDE - 1)):
                slot = lax.rem(place[kind] + SIDE - along, SIDE)
                ring_copy(kind, slot, pl.ds(n * half, half), n, 2 + n)

    def pick(_):
        to_smem.wait()
        tables_out.wait()
        for kind in (K, V):
            for n in (0, 1):
                await_bytes(ring[kind].at[0, pl.ds(0, half)], r_recv.at[kind, 2 + n])
        for n, (cross, cores) in enumerate(HOPS):
            for kind in (K, V):
                dest = crossing(kind, 0, cross, cores)
                for a in range(SIDE):
                    picked[kind, n, a] = ring[kind][a, wanted[kind * SIDE + a, dest[0] * span_tiles]]
                remote(
                    picked.at[kind, n], bank[kind].at[pl.ds((place[1 - kind] * CORES + core) * SIDE, SIDE)],
                    b_send.at[kind], b_recv.at[kind], dest,
                )
        for kind in (K, V):
            for a in range(SIDE):
                bank[kind][(place[1 - kind] * CORES + core) * SIDE + a] = ring[kind][
                    a, wanted[kind * SIDE + a, s * span_tiles]
                ]

    def attend(_):
        for o in range(1, n_head):
            arrived(Q, o)
        for kind in (K, V):
            await_bytes(bank[kind].at[pl.ds(0, len(HOPS) * SIDE)], b_recv.at[kind])

        @pl.loop(0, span_tiles)
        def _(step):
            i = step
            row = s * span_tiles + i
            mate = i + 1 - 2 * (i % 2)
            keys = [ring_k[place[K], i], ring_k[place[K], mate]]
            vals = [ring_v[place[V], i], ring_v[place[V], mate]]
            for e in range(2, slots):
                keys.append(bank_k[look[1, e, row]])
                vals.append(bank_v[look[2, e, row]])
            rows, inv = softmax(blk_q[i], keys, key_bias(row))
            mixed = jnp.dot(rows, jnp.concatenate(vals, axis=0), preferred_element_type=jnp.float32)
            blk_out[i] = (mixed * inv).astype(jnp.bfloat16)

    def answer(_):
        for o in (2, 1, 3):
            dest = lax.rem(x + o, n_head)
            remote(
                blk_out.at[pl.ds(dest * own_tiles, own_tiles)], o_ref.at[:, :, columns(rest_head)],
                o_send.at[2], o_recv.at[2], beside(o),
            )
        pltpu.make_async_copy(blk_out.at[mine], o_ref.at[:, :, columns(rest_head)], o_own.at[0]).start()

    stages = dict(
        send=send, scale=scale, look_up=look_up, answer=answer, own=own, early=early, spread_k=spread_k, spread_v=spread_v, halve=halve, join=join, spread_q=spread_q,
        own_ring=own_ring, direct=direct, pass_on=pass_on, finish=finish, complete=complete,
        ring_rest=ring_rest, relay=relay, pick=pick, weigh=weigh, attend=attend, mix=mix,
    )
    for name, *args in schedule():
        stages[name](*args)

    away = pl.ds(0, (COLUMNS - 1) * own_tiles)
    aside = blk_q.at[pl.ds(0, span_tiles - own_tiles)]
    for kind in (K, V, Q, W):
        await_bytes((col_k if kind == Q else col[kind]).at[away], m_send.at[kind])
    for kind in (K, V, Q):
        await_bytes(aside, a_send.at[kind])
    for kind in (K, V, W):
        await_bytes(col[kind].at[slab(0, 0, 3 * COLUMNS, 0)], x_send.at[kind])
        await_bytes(col[kind].at[slab(0, 0, n_head * COLUMNS, 0)], c_send.at[kind])
    for kind in (K, V):
        await_bytes(ring_k.at[pl.ds(0, 3)], r_send.at[kind])
        await_bytes(picked.at[kind], b_send.at[kind])
    for n in (0, 1):
        await_bytes(landed.at[0, pl.ds(0, COLUMNS - 1)], o_send.at[n])
    await_bytes(aside, o_send.at[2])
    await_bytes(aside, o_recv.at[2])
    pltpu.make_async_copy(blk_out.at[mine], o_ref.at[:, :, columns(rest_head)], o_own.at[0]).wait()


def on_device(queries, keys, values, gain_q, gain_k, key_tiles, tile_counts, tile_valid):
    n_head = lax.axis_size("head")
    rows, width = queries.shape
    own_tiles = rows // TILE
    span_tiles = own_tiles * n_head
    heads = width // HD
    tiles, slots = key_tiles.shape
    listed = key_tiles.T

    hbm = pl.BlockSpec(memory_space=pl.ANY)
    shape = (own_tiles, TILE, width)
    dma = pltpu.SemaphoreType.DMA

    def buffer(*lead, tail=(TILE, HD), kind=jnp.bfloat16):
        return pltpu.VMEM((*lead, *tail), kind)

    out = pl.pallas_call(
        functools.partial(kernel, n_head),
        out_shape=pltpu.VMEM(shape, jnp.bfloat16),
        in_specs=[hbm] * 8,
        out_specs=pl.BlockSpec(memory_space=pltpu.VMEM),
        scratch_shapes=[
            pltpu.SMEM((tiles,), jnp.int32),
            pltpu.VMEM((width,), jnp.float32),
            pltpu.VMEM((width,), jnp.float32),
            pltpu.VMEM((slots, tiles), jnp.int32),
            pltpu.VMEM((tiles,), jnp.int32),
            pltpu.SemaphoreType.DMA((5,)),
            pltpu.VMEM(shape, jnp.bfloat16),
            pltpu.VMEM(shape, jnp.bfloat16),
            pltpu.VMEM(shape, jnp.bfloat16),
            buffer(heads, own_tiles),
            buffer(heads, own_tiles),
            buffer(2, COLUMNS, own_tiles, tail=(HALF, HD)),
            pltpu.VMEM((2 * SIDE, tiles), jnp.int32),
            pltpu.SMEM((2 * SIDE, tiles), jnp.int32),
            pltpu.VMEM((4, slots, tiles), jnp.int32),
            pltpu.SMEM((4, slots, tiles), jnp.int32),
            buffer(tiles),
            buffer(tiles, tail=(HALF, HD)),
            buffer(tiles, tail=(HALF, HD)),
            buffer(COLUMNS, own_tiles),
            buffer(2, COLUMNS),
            buffer(2, COLUMNS),
            buffer(COLUMNS, own_tiles, tail=(TILE, slots * TILE)),
            buffer(COLUMNS, own_tiles, tail=(TILE, 1), kind=jnp.float32),
            buffer(SIDE, span_tiles),
            buffer(SIDE, span_tiles),
            buffer(SIDE * CORES * SIDE),
            buffer(SIDE * CORES * SIDE),
            buffer(span_tiles),
            buffer(2, len(HOPS), SIDE),
            buffer(span_tiles),
            dma((4,)),
            dma((2,)),
            dma((4,)),
            dma((4, SIDE)),
            dma((4,)),
            dma((4, 4, SIDE)),
            dma((4,)),
            dma((4,)),
            dma((3,)),
            dma((3, n_head - 1)),
            dma((2,)),
            dma((2, 4)),
            dma((2,)),
            dma((2,)),
            dma((3,)),
            dma((3,)),
            dma((1,)),
        ],
        compiler_params=pltpu.CompilerParams(
            collective_id=0, has_side_effects=True, vmem_limit_bytes=58 << 20
        ),
    )(
        tile_valid,
        queries.reshape(shape), keys.reshape(shape), values.reshape(shape),
        gain_q, gain_k, listed, tile_counts,
    )
    return out.reshape(rows, width)


def solution(mesh):
    placed = P(("seq", "head"), None)
    return jax.shard_map(
        on_device,
        mesh=mesh,
        in_specs=(placed, placed, placed, P(), P(), P(), P(), P()),
        out_specs=placed,
        check_vma=False,
    )
```
